128 devices in a mesh: seq: 16 (over y, x_lo, core), chan: 8 (over z, x_hi).
Axes of the slice: x: 4 (x_hi: 2, x_lo: 2; x = x_hi * 2 + x_lo), y: 4, z: 4, core: 2. Of those that a mesh axis runs over, the one named last changes fastest.
Arguments:
- signal: bfloat16 [512, 65536], P('chan', 'seq'), may hold values from -6 to 6
- gate: bfloat16 [512, 65536], P('chan', 'seq'), may hold values from -6 to 6
- spec_real: float32 [512, 32, 4096], P('chan', 'seq'), may hold values from -6 to 6
- spec_imag: float32 [512, 32, 4096], P('chan', 'seq'), may hold values from -6 to 6
- skip_gain: float32 [512], P('chan'), may hold values from 0.5 to 1.5
- mix_weight: bfloat16 [512, 512], P('chan'), may hold values from -0.25 to 0.25
Outputs:
- mixed: bfloat16 [512, 65536], P('chan', 'seq')
The draws below stay inside these ranges and needn't reach their ends.
All inputs are finite; a program needn't handle non-finite values.
Results may differ from the reference program's by a relative error of at most 0.0049.
Values may be sent and summed in bfloat16 or wider, within the bound.
A program may use at most 128 MiB of HBM per device.

```python
import jax
import jax.numpy as jnp
from jax import lax

RESID = 32
SEQ = 65536
INNER = 4096
CHANNELS = 512


def level_of(own_key, extent, split, least, largest):
    loudness = 1.0
    for axis_at, parts in split:
        steps = jax.random.uniform(jax.random.fold_in(jax.random.fold_in(own_key, 6), axis_at), (parts,), jnp.float32, least / len(split), largest / len(split))
        loudness = loudness * jnp.repeat(jnp.exp(steps), extent[axis_at] // parts).reshape((-1,) + (1,) * (len(extent) - 1 - axis_at))
    return loudness


def scatter_about(own_key, shape, width, limit, split=(), held_as=jnp.bfloat16):
    loudness = level_of(own_key, shape, split, -0.22, 0.18) if split else 1.0
    entries = jax.random.normal(own_key, shape, jnp.float32) * width * loudness
    return jnp.minimum(jnp.maximum(entries, -limit), limit).astype(held_as)


def setup_inputs(seed: int = 0) -> dict:
    splits = jax.random.split(jax.random.key(seed), 7)
    return {
        "signal": scatter_about(splits[0], (CHANNELS, SEQ), 1.0, 6.0, ((0, 8), (1, 16))),
        "gate": scatter_about(splits[1], (CHANNELS, SEQ), 1.0, 6.0, ((0, 8), (1, 16))),
        "spec_real": scatter_about(splits[2], (CHANNELS, RESID, INNER), 1.0, 6.0, ((0, 8), (1, 16)), jnp.float32),
        "spec_imag": scatter_about(splits[3], (CHANNELS, RESID, INNER), 1.0, 6.0, ((0, 8), (1, 16)), jnp.float32),
        "skip_gain": jnp.clip(0.5 + 1.0 * jax.random.uniform(splits[4], (CHANNELS,), jnp.float32) ** level_of(splits[4], (CHANNELS,), ((0, 8),), -0.2, 0.2), 0.5, 1.5),
        "mix_weight": scatter_about(splits[5], (CHANNELS, CHANNELS), CHANNELS ** -0.5, 0.25, ((0, 8),)),
    }


def one_channel(packed):
    values, real_part, imag_part = packed
    wide = values.astype(jnp.float32)
    padded = jnp.concatenate([wide, jnp.zeros_like(wide)])
    spectrum = jnp.fft.fft(padded)
    filt = lax.complex(real_part.T.reshape(-1), imag_part.T.reshape(-1))
    inverse = jnp.fft.ifft(spectrum * filt)
    return jnp.real(inverse)[: values.shape[0]]


def reference(signal, gate, spec_real, spec_imag, skip_gain, mix_weight):
    conv = lax.map(one_channel, (signal, spec_real, spec_imag))
    direct = conv + skip_gain[:, None] * signal.astype(jnp.float32)
    gated = (gate.astype(jnp.float32) * direct).astype(jnp.bfloat16)
    return jnp.dot(mix_weight, gated, preferred_element_type=jnp.float32).astype(jnp.bfloat16)
```

```python
import functools

import jax
import jax.numpy as jnp
import numpy as np
from jax import lax
from jax.experimental import pallas as pl
from jax.experimental.pallas import tpu as pltpu
from jax.sharding import PartitionSpec as P

BF = jnp.bfloat16
F32 = jnp.float32
N = 131072


def unit(numer, period):
    angle = 2.0 * np.pi * (np.asarray(numer, np.int64) % period) / period
    return np.cos(angle), np.sin(angle)


def tables():
    r = np.arange(32)
    a = np.arange(16)
    i, h, jb = np.meshgrid(np.arange(4), np.arange(2), np.arange(16), indexing="ij")
    s1 = (4 * (16 * h + jb) + i).reshape(-1)
    m2 = np.arange(128)
    m1 = np.arange(32)
    s2 = np.arange(32)
    eye16 = np.eye(16)
    eye4 = np.eye(4)
    c, s = unit(r[:, None] * a[None, :], 32)
    k0 = np.concatenate([np.kron(c, eye16), np.kron(-s, eye16)], 0)
    k0i = np.concatenate([np.kron(c.T, eye16), np.kron(-s.T, eye16)], 1)
    klow = 32 * m2[None, :] + r[:, None]
    c, s = unit(klow[:, :, None] * s1[None, None, :], 4096)
    m = np.concatenate([np.concatenate([c, s], 2), np.concatenate([-s, c], 2)], 1)
    mi = np.swapaxes(m, 1, 2)
    c, s = unit(klow[:, :, None] * np.tile(s2, 4)[None, None, :], N)
    tw = np.stack([c, s], 1)
    twi = np.swapaxes(tw, 2, 3)
    c, s = unit(m1[:, None] * s2[None, :], 32)
    c, s = np.kron(eye4, c), np.kron(eye4, s)
    l2 = np.concatenate([np.concatenate([c, s], 1), np.concatenate([-s, c], 1)], 0)
    l2i = l2.T
    perm = np.zeros((4, 4, 32, 4, 4, 32))
    for ci in range(4):
        for ii in range(4):
            perm[ci, ii, np.arange(32), ii, ci, np.arange(32)] = 1
    perm = perm.reshape(512, 512)
    return dict(k0=k0, k0i=k0i / N, m=m, mi=mi, tw=tw, twi=twi, l2=l2, l2i=l2i, perm=perm)


def split(x):
    x = np.asarray(x, np.float32)
    hi = x.astype(jnp.bfloat16)
    lo = (x - hi.astype(np.float32)).astype(jnp.bfloat16)
    return hi, lo


def dot(a, b):
    return lax.dot_general(a, b, (((1,), (0,)), ((), ())), preferred_element_type=F32)


def dot_nt(a, b):
    return lax.dot_general(a, b, (((1,), (1,)), ((), ())), preferred_element_type=F32)


def conv_kernel(x_ref, hre_ref, him_ref, k0_ref, k0i_ref, m_ref, mi_ref, tw_ref, twi_ref,
                l2_ref, l2i_ref, perm_ref, permi_ref, out_ref, dsc, osc):
    xa = jnp.concatenate([x_ref[:, c].reshape(512, 128) for c in range(4)], axis=1)
    spread = dot(xa, perm_ref[...]).astype(BF).reshape(16, 32, 512)
    for h in range(2):
        rows = spread[:, h * 16:(h + 1) * 16].reshape(256, 512)
        d = (dot(k0_ref[0], rows) + dot(k0_ref[1], rows)).astype(BF)
        for ri in range(2):
            for i in range(4):
                dsc[:, pl.ds(ri * 128 + i * 32 + h * 16, 16), :] = d[
                    ri * 512:(ri + 1) * 512, i * 128:(i + 1) * 128].reshape(32, 16, 128)

    def one(r):
        e = dot(m_ref[r], dsc[r])
        er, ei = e[:128], e[128:]
        c, s = tw_ref[r, 0], tw_ref[r, 1]
        ec = jnp.concatenate([er * c + ei * s, ei * c - er * s], axis=1).astype(BF)
        f = dot_nt(l2_ref[...], ec)
        fr, fi = f[:128], f[128:]
        hr, hi = hre_ref[r].astype(F32), him_ref[r].astype(F32)
        p = jnp.concatenate([fr * hr - fi * hi, fr * hi + fi * hr], axis=0).astype(BF)
        g = dot(l2i_ref[...], p)
        gr, gi = g[:128], g[128:]
        c, s = twi_ref[r, 0], twi_ref[r, 1]
        gc = jnp.concatenate([gr * c - gi * s, gi * c + gr * s], axis=1).astype(BF)
        o = dot_nt(mi_ref[r], gc).astype(BF)
        for ri in range(2):
            for i in range(4):
                for h in range(2):
                    osc[h, pl.ds(pl.multiple_of(ri * 512 + r * 16, 16), 16), pl.ds(i * 128, 128)] = (
                        o[ri * 128 + i * 32 + h * 16:ri * 128 + i * 32 + h * 16 + 16])

    def step(t, carry):
        for u in range(4):
            one(t * 4 + u)
        return carry

    lax.fori_loop(0, 8, step, 0)
    halves = []
    for h in range(2):
        back = dot(k0i_ref[0], osc[h]) + dot(k0i_ref[1], osc[h])
        halves.append((back * (1.0 / N)).astype(BF))
    for h in range(2):
        y = dot(halves[h], permi_ref[...]).astype(BF).reshape(16, 16, 512)
        for c in range(4):
            out_ref[:, c, pl.ds(h * 16, 16), :] = y[:, :, c * 128:(c + 1) * 128]


def constants():
    t = tables()
    pair = lambda v: np.stack(split(v))
    one = lambda v: np.asarray(v, np.float32).astype(jnp.bfloat16)
    f = lambda v: np.asarray(v, np.float32)
    return [pair(t["k0"]), pair(t["k0i"] * N), one(t["m"]), one(t["mi"]), f(t["tw"]), f(t["twi"]),
            one(t["l2"]), one(t["l2i"]), one(t["perm"]), one(t["perm"].T)]


def conv_local(x, hre, him, interpret=False):
    consts = [jnp.asarray(v) for v in constants()]
    return pl.pallas_call(
        conv_kernel,
        out_shape=jax.ShapeDtypeStruct((16, 4, 32, 128), BF),
        in_specs=[pl.BlockSpec(memory_space=pltpu.VMEM)] * 13,
        out_specs=pl.BlockSpec(memory_space=pltpu.VMEM),
        scratch_shapes=[pltpu.VMEM((32, 256, 128), BF), pltpu.VMEM((2, 1024, 512), BF)],
        compiler_params=pltpu.CompilerParams(vmem_limit_bytes=56 * 1024 * 1024),
        cost_estimate=pl.CostEstimate(flops=10**10, bytes_accessed=2 * 10**7, transcendentals=0),
        interpret=interpret,
    )(x, hre, him, *consts)


def body(signal, gate, spec_real, spec_imag, skip_gain, mix_weight):
    swap = functools.partial(lax.all_to_all, axis_name="seq", split_axis=0, concat_axis=0)
    x = swap(signal.reshape(4, 16, 32, 128).transpose(1, 0, 2, 3))
    deal = lambda v: swap(
        v.reshape(4, 16, 2, 32, 128).transpose(1, 2, 0, 3, 4).astype(BF).reshape(16, 256, 128)
    ).reshape(32, 128, 128)
    conv = swap(conv_local(x, deal(spec_real), deal(spec_imag)))
    conv = conv.transpose(1, 0, 2, 3).reshape(64, 4096).astype(F32)
    direct = conv + skip_gain[:, None] * signal.astype(F32)
    gated = (gate.astype(F32) * direct).astype(BF)
    result = jnp.dot(
        mix_weight,
        lax.all_gather(gated, "chan", axis=0, tiled=True),
        preferred_element_type=F32,
    )
    return result.astype(BF)


def solution(mesh):
    placed = (
        P("chan", "seq"),
        P("chan", "seq"),
        P("chan", "seq", None),
        P("chan", "seq", None),
        P("chan"),
        P("chan", None),
    )
    return jax.shard_map(
        body, mesh=mesh, in_specs=placed, out_specs=P("chan", "seq"), check_vma=False
    )
```

```python
import jax
import jax.numpy as jnp
import numpy as np
from jax import lax
from jax.experimental import pallas as pl
from jax.experimental.pallas import tpu as pltpu
from jax.sharding import PartitionSpec as P

BF = jnp.bfloat16
F32 = jnp.float32
N = 131072
SEQ_N = 16
CHAN_N = 8
MESH = pl.DeviceIdType.MESH


def unit(numer, period):
    angle = 2.0 * np.pi * (np.asarray(numer, np.int64) % period) / period
    return np.cos(angle), np.sin(angle)


def tables():
    r = np.arange(32)
    a = np.arange(16)
    i, h, jb = np.meshgrid(np.arange(4), np.arange(2), np.arange(16), indexing="ij")
    s1 = (4 * (16 * h + jb) + i).reshape(-1)
    m2 = np.arange(128)
    m1 = np.arange(32)
    s2 = np.arange(32)
    eye16 = np.eye(16)
    eye4 = np.eye(4)
    c, s = unit(r[:, None] * a[None, :], 32)
    k0 = np.concatenate([np.kron(c, eye16), np.kron(-s, eye16)], 0)
    k0i = np.concatenate([np.kron(c.T, eye16), np.kron(-s.T, eye16)], 1)
    klow = 32 * m2[None, :] + r[:, None]
    c, s = unit(klow[:, :, None] * s1[None, None, :], 4096)
    m = np.concatenate([np.concatenate([c, s], 2), np.concatenate([-s, c], 2)], 1)
    mi = np.swapaxes(m, 1, 2)
    c, s = unit(klow[:, :, None] * np.tile(s2, 4)[None, None, :], N)
    tw = np.stack([c, s], 1)
    twi = np.swapaxes(tw, 2, 3)[:, :, :64]
    c, s = unit(m1[:, None] * s2[None, :], 32)
    c, s = np.kron(eye4, c), np.kron(eye4, s)
    l2 = np.concatenate([np.concatenate([c, s], 1), np.concatenate([-s, c], 1)], 0)
    c, s = unit(s2[:, None] * m1[None, :], 32)
    c, s = np.kron(np.eye(2), c), np.kron(np.eye(2), s)
    l2i = np.concatenate([np.concatenate([c, -s], 1), np.concatenate([s, c], 1)], 0)
    perm = np.zeros((4, 4, 32, 4, 4, 32))
    for ci in range(4):
        for ii in range(4):
            perm[ci, ii, np.arange(32), ii, ci, np.arange(32)] = 1
    perm = perm.reshape(512, 512)
    permi = np.zeros((4, 2, 32, 2, 4, 32))
    for ci in range(2):
        for ii in range(4):
            permi[ii, ci, np.arange(32), ci, ii, np.arange(32)] = 1
    permi = permi.reshape(256, 256)
    return k0, k0i, m, mi, tw, twi, l2, l2i, perm, permi


def split(x):
    x = np.asarray(x, np.float32)
    hi = x.astype(jnp.bfloat16)
    lo = (x - hi.astype(np.float32)).astype(jnp.bfloat16)
    return hi, lo


def constants():
    k0, k0i, m, mi, tw, twi, l2, l2i, perm, permi = tables()
    pair = lambda v: np.stack(split(v))
    one = lambda v: np.asarray(v, np.float32).astype(jnp.bfloat16)
    f = lambda v: np.asarray(v, np.float32)
    return [pair(k0), pair(k0i), one(m), one(mi), f(tw), f(twi), one(l2), one(l2i), one(perm), one(permi)]


def dot(a, b):
    return lax.dot_general(a, b, (((1,), (0,)), ((), ())), preferred_element_type=F32)


def dot_nt(a, b):
    return lax.dot_general(a, b, (((1,), (1,)), ((), ())), preferred_element_type=F32)


def kernel(sig_hbm, gate_hbm, hre_hbm, him_hbm, gain_ref, w_ref,
           k0_hbm, k0i_hbm, m_hbm, mi_hbm, tw_hbm, twi_hbm, l2_hbm, l2i_hbm, perm_hbm, permi_hbm,
           out_ref,
           sig, gate, h32, k0, k0i, m, mi, tw, twi, l2, l2i, perm, permi,
           s32, sx, xr, hs, hr, dsc, fsc, osc, cs, cr, c32, gt, acc,
           load_sem, xs_sem, xr_sem, hs_sem, hr_sem, cs_sem, cr_sem, gs_sem, gr_sem):
    me = lax.axis_index("seq")
    mc = lax.axis_index("chan")
    peer = [lax.rem(me + d, SEQ_N) for d in range(SEQ_N)]
    source = [lax.rem(me - d + SEQ_N, SEQ_N) for d in range(SEQ_N)]
    other = [lax.rem(mc + d, CHAN_N) for d in range(CHAN_N)]
    origin = [lax.rem(mc - d + CHAN_N, CHAN_N) for d in range(CHAN_N)]

    barrier = pltpu.get_barrier_semaphore()
    for d in range(1, SEQ_N):
        pl.semaphore_signal(barrier, inc=1, device_id=(peer[d], mc), device_id_type=MESH)
    for d in range(1, CHAN_N):
        pl.semaphore_signal(barrier, inc=1, device_id=(me, other[d]), device_id_type=MESH)

    pairs = [(sig_hbm, sig), (hre_hbm, h32.at[0]), (him_hbm, h32.at[1]), (perm_hbm, perm), (k0_hbm, k0),
             (m_hbm, m), (l2_hbm, l2), (tw_hbm, tw), (l2i_hbm, l2i), (twi_hbm, twi), (mi_hbm, mi),
             (k0i_hbm, k0i), (permi_hbm, permi), (gate_hbm, gate)]
    loads = [pltpu.make_async_copy(a, b, load_sem.at[n]) for n, (a, b) in enumerate(pairs)]
    for copy in loads:
        copy.start()

    loads[0].wait()
    for c in range(4):
        for j in range(32):
            s32[c, pl.ds(j, 16, stride=32), :] = sig[c * 16:(c + 1) * 16, j * 128:(j + 1) * 128].astype(F32)
    for c in range(4):
        sx[:, c] = s32[c].astype(BF).reshape(16, 32, 128)
    pl.semaphore_wait(barrier, SEQ_N + CHAN_N - 2)
    x_out = []
    for d in range(1, SEQ_N):
        copy = pltpu.make_async_remote_copy(
            src_ref=sx.at[peer[d]], dst_ref=xr.at[me], send_sem=xs_sem.at[d], recv_sem=xr_sem.at[d],
            device_id=(peer[d], mc), device_id_type=MESH)
        copy.start()
        x_out.append(copy)
    xr[me] = sx[me]

    loads[1].wait()
    loads[2].wait()
    h_out = []
    for g in range(2):
        for d in list(range(1, SEQ_N)) + [0]:
            for part in range(2):
                for i in range(2):
                    for cl in range(2):
                        row = pl.multiple_of(((2 * g + cl) * 16 + peer[d]) * 64, 64) + i
                        val = h32[part, pl.ds(row, 32, stride=2), :].astype(BF)
                        if d == 0:
                            hr[g, me, part, i, pl.ds(cl * 32, 32), :] = val
                        else:
                            hs[g, d, part, i, pl.ds(cl * 32, 32), :] = val
            if d:
                copy = pltpu.make_async_remote_copy(
                    src_ref=hs.at[g, d], dst_ref=hr.at[g, me], send_sem=hs_sem.at[g, d],
                    recv_sem=hr_sem.at[g, d], device_id=(peer[d], mc), device_id_type=MESH)
                copy.start()
                h_out.append(copy)

    for n in range(3, 8):
        loads[n].wait()
    for copy in x_out:
        copy.wait_recv()
    xa = jnp.concatenate([xr[:, c].reshape(512, 128) for c in range(4)], axis=1)
    spread = dot(xa, perm[...]).astype(BF).reshape(16, 32, 512)
    for h in range(2):
        rows = spread[:, h * 16:(h + 1) * 16].reshape(256, 512)
        dv = (dot(k0[0], rows) + dot(k0[1], rows)).astype(BF)
        for ri in range(2):
            for i in range(4):
                dsc[:, pl.ds(ri * 128 + i * 32 + h * 16, 16), :] = dv[
                    ri * 512:(ri + 1) * 512, i * 128:(i + 1) * 128].reshape(32, 16, 128)

    def forward(t, carry):
        ecs = []
        for u in range(4):
            r = t * 4 + u
            e = dot(m[r], dsc[r])
            er, ei = e[:128], e[128:]
            c, s = tw[r, 0], tw[r, 1]
            ecs.append(jnp.concatenate([er * c + ei * s, ei * c - er * s], axis=1).astype(BF))
        for u in range(0, 4, 2):
            f = dot_nt(l2[...], jnp.concatenate(ecs[u:u + 2], axis=0))
            fsc[t * 4 + u] = f[:, :128]
            fsc[t * 4 + u + 1] = f[:, 128:]
        return carry

    lax.fori_loop(0, 8, forward, 0)
    for n in range(8, 14):
        loads[n].wait()
    low = lax.broadcasted_iota(jnp.int32, (32, 128), 1) < 64

    def inverse_of(g, q):
        ps = []
        for i in range(2):
            r = 2 * q + i
            fr = fsc[r, pl.ds(g * 64, 64), :]
            fi = fsc[r, pl.ds(128 + g * 64, 64), :]
            re, im = hr[g, q, 0, i].astype(F32), hr[g, q, 1, i].astype(F32)
            ps.append(jnp.concatenate([fr * re - fi * im, fr * im + fi * re], axis=0).astype(BF))
        gv = dot(l2i[...], jnp.concatenate(ps, axis=1))
        for i in range(2):
            r = 2 * q + i
            gr, gi = gv[:64, i * 128:(i + 1) * 128], gv[64:, i * 128:(i + 1) * 128]
            c, s = twi[r, 0], twi[r, 1]
            gc = jnp.concatenate([gr * c - gi * s, gi * c + gr * s], axis=1).astype(BF)
            o = dot_nt(mi[r], jnp.concatenate([gc, gc], axis=0))
            for ri in range(2):
                for k in range(2):
                    at = ri * 128 + k * 64
                    val = jnp.where(low, o[at:at + 32], o[at + 32:at + 64]).astype(BF)
                    for h in range(2):
                        osc[g, h, pl.ds(pl.multiple_of(ri * 512 + r * 16, 16), 16), pl.ds(k * 128, 128)] = (
                            val[h * 16:(h + 1) * 16])

    def inverse_step(g):
        def step(d, carry):
            q = lax.rem(me - d + SEQ_N, SEQ_N)
            pltpu.make_async_remote_copy(
                src_ref=hs.at[g, d], dst_ref=hr.at[g, q], send_sem=hs_sem.at[g, d],
                recv_sem=hr_sem.at[g, d], device_id=(me, mc), device_id_type=MESH).wait_recv()
            inverse_of(g, q)
            return carry
        return step

    def inverse_end(g):
        for h in range(2):
            back = dot(k0i[0], osc[g, h]) + dot(k0i[1], osc[g, h])
            y = dot((back * (1.0 / N)).astype(BF), permi[...]).astype(BF).reshape(16, 16, 256)
            for cl in range(2):
                cs[g, :, cl, pl.ds(h * 16, 16), :] = y[:, :, cl * 128:(cl + 1) * 128]
        sent = []
        for d in range(1, SEQ_N):
            copy = pltpu.make_async_remote_copy(
                src_ref=cs.at[g, peer[d]], dst_ref=cr.at[g, me], send_sem=cs_sem.at[g, d],
                recv_sem=cr_sem.at[g, d], device_id=(peer[d], mc), device_id_type=MESH)
            copy.start()
            sent.append(copy)
        cr[g, me] = cs[g, me]
        return sent

    def gating(g, arrivals):
        for copy in arrivals:
            copy.wait_recv()
        for cl in range(2):
            c32[cl] = cr[g, :, cl].reshape(512, 128).astype(F32)
        for cl in range(2):
            at = (2 * g + cl) * 16
            gain = gain_ref[at:at + 16, :]
            for j in range(32):
                lanes = slice(j * 128, (j + 1) * 128)
                direct = c32[cl, pl.ds(j, 16, stride=32), :] + gain * sig[at:at + 16, lanes].astype(F32)
                gt[g, mc, pl.ds(cl * 16, 16), lanes] = (gate[at:at + 16, lanes].astype(F32) * direct).astype(BF)
        sent = []
        for d in range(1, CHAN_N):
            copy = pltpu.make_async_remote_copy(
                src_ref=gt.at[g, mc], dst_ref=gt.at[g, mc], send_sem=gs_sem.at[g, d],
                recv_sem=gr_sem.at[g, d], device_id=(me, other[d]), device_id_type=MESH)
            copy.start()
            sent.append(copy)
        return sent

    inverse_of(0, me)
    lax.fori_loop(1, SEQ_N, inverse_step(0), 0)
    conv_a = inverse_end(0)
    inverse_of(1, me)
    lax.fori_loop(1, 9, inverse_step(1), 0)
    gather_a = gating(0, conv_a)
    lax.fori_loop(9, SEQ_N, inverse_step(1), 0)
    conv_b = inverse_end(1)
    gather_b = gating(1, conv_b)

    def mixing(g, arrivals):
        for copy in arrivals:
            copy.wait_recv()
        for j in range(8):
            lanes = slice(j * 512, (j + 1) * 512)
            part = dot(w_ref[g], gt[g, :, :, lanes].reshape(32 * CHAN_N, 512))
            if g == 0:
                acc[:, lanes] = part
            else:
                out_ref[:, lanes] = (acc[:, lanes] + part).astype(BF)

    mixing(0, gather_a)
    mixing(1, gather_b)
    for copy in x_out + h_out + conv_a + conv_b + gather_a + gather_b:
        copy.wait_send()


def body(signal, gate, spec_real, spec_imag, skip_gain, mix_weight):
    consts = [jnp.asarray(v) for v in constants()]
    rows = lambda v: v.reshape(64, 2, 32, 128).transpose(0, 2, 1, 3).reshape(4096, 128)
    gain = jnp.broadcast_to(skip_gain[:, None], (64, 128))
    weight = mix_weight.reshape(64, CHAN_N, 2, 32).transpose(2, 0, 1, 3).reshape(2, 64, 32 * CHAN_N)
    anywhere = pl.BlockSpec(memory_space=pl.ANY)
    vmem = pl.BlockSpec(memory_space=pltpu.VMEM)
    buf = lambda *shape: pltpu.VMEM(shape, BF)
    wide = lambda *shape: pltpu.VMEM(shape, F32)
    dma = lambda *shape: pltpu.SemaphoreType.DMA(shape)
    held = [pltpu.VMEM(v.shape, v.dtype) for v in consts]
    return pl.pallas_call(
        kernel,
        out_shape=jax.ShapeDtypeStruct((64, 4096), BF),
        in_specs=[anywhere] * 4 + [vmem] * 2 + [anywhere] * len(consts),
        out_specs=vmem,
        scratch_shapes=[buf(64, 4096), buf(64, 4096), wide(2, 4096, 128)] + held + [
            wide(4, 512, 128), buf(16, 4, 32, 128), buf(16, 4, 32, 128),
            buf(2, 16, 2, 2, 64, 128), buf(2, 16, 2, 2, 64, 128), buf(32, 256, 128), wide(32, 256, 128),
            buf(2, 2, 1024, 256), buf(2, 16, 2, 32, 128), buf(2, 16, 2, 32, 128), wide(2, 512, 128),
            buf(2, CHAN_N, 32, 4096), wide(64, 4096),
            dma(14), dma(16), dma(16), dma(2, 16), dma(2, 16), dma(2, 16), dma(2, 16), dma(2, 8), dma(2, 8)],
        compiler_params=pltpu.CompilerParams(
            collective_id=0, has_side_effects=True, vmem_limit_bytes=60 * 1024 * 1024),
        cost_estimate=pl.CostEstimate(flops=10**10, bytes_accessed=3 * 10**7, transcendentals=0),
    )(signal, gate, rows(spec_real), rows(spec_imag), gain, weight, *consts)


def solution(mesh):
    placed = (
        P("chan", "seq"),
        P("chan", "seq"),
        P("chan", "seq", None),
        P("chan", "seq", None),
        P("chan"),
        P("chan", None),
    )
    return jax.shard_map(
        body, mesh=mesh, in_specs=placed, out_specs=P("chan", "seq"), check_vma=False
    )
```

```python
import jax
import jax.numpy as jnp
import numpy as np
from jax import lax
from jax.experimental import pallas as pl
from jax.experimental.pallas import tpu as pltpu
from jax.sharding import PartitionSpec as P

BF = jnp.bfloat16
F32 = jnp.float32
N = 131072
SEQ_N = 16
CHAN_N = 8
MESH = pl.DeviceIdType.MESH


def unit(numer, period):
    angle = 2.0 * np.pi * (np.asarray(numer, np.int64) % period) / period
    return np.cos(angle), np.sin(angle)


def tables():
    r = np.arange(32)
    a = np.arange(16)
    i, h, jb = np.meshgrid(np.arange(4), np.arange(2), np.arange(16), indexing="ij")
    s1 = (4 * (16 * h + jb) + i).reshape(-1)
    m2 = np.arange(128)
    m1 = np.arange(32)
    s2 = np.arange(32)
    eye16 = np.eye(16)
    eye4 = np.eye(4)
    c, s = unit(r[:, None] * a[None, :], 32)
    k0 = np.concatenate([np.kron(c, eye16), np.kron(-s, eye16)], 0)
    k0i = np.concatenate([np.kron(c.T, eye16), np.kron(-s.T, eye16)], 1)
    klow = 32 * m2[None, :] + r[:, None]
    c, s = unit(klow[:, :, None] * s1[None, None, :], 4096)
    m = np.concatenate([np.concatenate([c, s], 2), np.concatenate([-s, c], 2)], 1)
    mi = np.swapaxes(m, 1, 2)
    c, s = unit(klow[:, :, None] * np.tile(s2, 4)[None, None, :], N)
    tw = np.stack([c, s], 1)
    twi = np.swapaxes(tw, 2, 3)[:, :, :64]
    c, s = unit(m1[:, None] * s2[None, :], 32)
    c, s = np.kron(eye4, c), np.kron(eye4, s)
    l2 = np.concatenate([np.concatenate([c, s], 1), np.concatenate([-s, c], 1)], 0)
    c, s = unit(s2[:, None] * m1[None, :], 32)
    c, s = np.kron(np.eye(2), c), np.kron(np.eye(2), s)
    l2i = np.concatenate([np.concatenate([c, -s], 1), np.concatenate([s, c], 1)], 0)
    perm = np.zeros((4, 4, 32, 4, 4, 32))
    for ci in range(4):
        for ii in range(4):
            perm[ci, ii, np.arange(32), ii, ci, np.arange(32)] = 1
    perm = perm.reshape(512, 512)
    permi = np.zeros((4, 2, 32, 2, 4, 32))
    for ci in range(2):
        for ii in range(4):
            permi[ii, ci, np.arange(32), ci, ii, np.arange(32)] = 1
    permi = permi.reshape(256, 256)
    return k0, k0i, m, mi, tw, twi, l2, l2i, perm, permi


def split(x):
    x = np.asarray(x, np.float32)
    hi = x.astype(jnp.bfloat16)
    lo = (x - hi.astype(np.float32)).astype(jnp.bfloat16)
    return hi, lo


def constants():
    k0, k0i, m, mi, tw, twi, l2, l2i, perm, permi = tables()
    pair = lambda v: np.stack(split(v))
    one = lambda v: np.asarray(v, np.float32).astype(jnp.bfloat16)
    f = lambda v: np.asarray(v, np.float32)
    return [pair(k0), pair(k0i), one(m), one(mi), f(tw), f(twi), one(l2), one(l2i), one(perm), one(permi)]


def dot(a, b):
    return lax.dot_general(a, b, (((1,), (0,)), ((), ())), preferred_element_type=F32)


def dot_nt(a, b):
    return lax.dot_general(a, b, (((1,), (1,)), ((), ())), preferred_element_type=F32)


def kernel(sig_hbm, gate_hbm, hre_hbm, him_hbm, gain_ref, w_ref,
           k0_hbm, k0i_hbm, m_hbm, mi_hbm, tw_hbm, twi_hbm, l2_hbm, l2i_hbm, perm_hbm, permi_hbm,
           out_ref,
           sig, gate, h32, k0, k0i, m, mi, tw, twi, l2, l2i, perm, permi,
           s32, sx, xr, hs, hr, dsc, fsc, osc, cs, cr, c32, gt,
           load_sem, xs_sem, xr_sem, hs_sem, hr_sem, cs_sem, cr_sem, gs_sem, gr_sem):
    me = lax.axis_index("seq")
    mc = lax.axis_index("chan")
    peer = [lax.rem(me + d, SEQ_N) for d in range(SEQ_N)]
    source = [lax.rem(me - d + SEQ_N, SEQ_N) for d in range(SEQ_N)]
    flip = lambda c: c + 1 - 2 * lax.rem(c, 2)
    pc = flip(mc)
    upc, dnc = lax.rem(mc + 2, CHAN_N), lax.rem(mc + 6, CHAN_N)

    barrier = pltpu.get_barrier_semaphore()
    for d in range(1, SEQ_N):
        pl.semaphore_signal(barrier, inc=1, device_id=(peer[d], mc), device_id_type=MESH)
    for c in (pc, upc, dnc):
        pl.semaphore_signal(barrier, inc=1, device_id=(me, c), device_id_type=MESH)

    pairs = [(sig_hbm, sig), (hre_hbm, h32.at[0]), (him_hbm, h32.at[1]), (perm_hbm, perm), (k0_hbm, k0),
             (m_hbm, m), (l2_hbm, l2), (tw_hbm, tw), (l2i_hbm, l2i), (twi_hbm, twi), (mi_hbm, mi),
             (k0i_hbm, k0i), (permi_hbm, permi), (gate_hbm, gate)]
    loads = [pltpu.make_async_copy(a, b, load_sem.at[n]) for n, (a, b) in enumerate(pairs)]
    for copy in loads:
        copy.start()

    square = lax.broadcasted_iota(jnp.int32, (64, 64), 0) == lax.broadcasted_iota(jnp.int32, (64, 64), 1)
    gain_col = jnp.sum(jnp.where(square, gain_ref[...], 0.0), axis=1, keepdims=True)

    loads[0].wait()
    for c in range(4):
        for j in range(32):
            s32[c, pl.ds(j, 16, stride=32), :] = sig[c * 16:(c + 1) * 16, j * 128:(j + 1) * 128].astype(F32)
    for c in range(4):
        sx[:, c] = s32[c].astype(BF).reshape(16, 32, 128)
    pl.semaphore_wait(barrier, SEQ_N + 2)
    x_out = []
    for d in range(1, SEQ_N):
        copy = pltpu.make_async_remote_copy(
            src_ref=sx.at[peer[d]], dst_ref=xr.at[me], send_sem=xs_sem.at[d], recv_sem=xr_sem.at[d],
            device_id=(peer[d], mc), device_id_type=MESH)
        copy.start()
        x_out.append(copy)
    xr[me] = sx[me]

    loads[1].wait()
    loads[2].wait()
    h_out = []
    for g in range(2):
        for d in list(range(1, SEQ_N)) + [0]:
            for part in range(2):
                for i in range(2):
                    for cl in range(2):
                        row = pl.multiple_of(((2 * g + cl) * 16 + peer[d]) * 64, 64) + i
                        val = h32[part, pl.ds(row, 32, stride=2), :].astype(BF)
                        if d == 0:
                            hr[g, me, part, i, pl.ds(cl * 32, 32), :] = val
                        else:
                            hs[g, d, part, i, pl.ds(cl * 32, 32), :] = val
            if d:
                copy = pltpu.make_async_remote_copy(
                    src_ref=hs.at[g, d], dst_ref=hr.at[g, me], send_sem=hs_sem.at[g, d],
                    recv_sem=hr_sem.at[g, d], device_id=(peer[d], mc), device_id_type=MESH)
                copy.start()
                h_out.append(copy)

    for n in range(3, 8):
        loads[n].wait()
    for copy in x_out:
        copy.wait_recv()
    xa = jnp.concatenate([xr[:, c].reshape(512, 128) for c in range(4)], axis=1)
    spread = dot(xa, perm[...]).astype(BF).reshape(16, 32, 512)
    for h in range(2):
        rows = spread[:, h * 16:(h + 1) * 16].reshape(256, 512)
        dv = (dot(k0[0], rows) + dot(k0[1], rows)).astype(BF)
        for ri in range(2):
            for i in range(4):
                dsc[:, pl.ds(ri * 128 + i * 32 + h * 16, 16), :] = dv[
                    ri * 512:(ri + 1) * 512, i * 128:(i + 1) * 128].reshape(32, 16, 128)

    def forward(t, carry):
        ecs = []
        for u in range(4):
            r = t * 4 + u
            e = dot(m[r], dsc[r])
            er, ei = e[:128], e[128:]
            c, s = tw[r, 0], tw[r, 1]
            ecs.append(jnp.concatenate([er * c + ei * s, ei * c - er * s], axis=1).astype(BF))
        for u in range(0, 4, 2):
            f = dot_nt(l2[...], jnp.concatenate(ecs[u:u + 2], axis=0))
            fsc[t * 4 + u] = f[:, :128]
            fsc[t * 4 + u + 1] = f[:, 128:]
        return carry

    lax.fori_loop(0, 8, forward, 0)
    for n in range(8, 14):
        loads[n].wait()
    low = lax.broadcasted_iota(jnp.int32, (32, 128), 1) < 64

    def inverse_of(g, q):
        ps = []
        for i in range(2):
            r = 2 * q + i
            fr = fsc[r, pl.ds(g * 64, 64), :]
            fi = fsc[r, pl.ds(128 + g * 64, 64), :]
            re, im = hr[g, q, 0, i].astype(F32), hr[g, q, 1, i].astype(F32)
            ps.append(jnp.concatenate([fr * re - fi * im, fr * im + fi * re], axis=0).astype(BF))
        gv = dot(l2i[...], jnp.concatenate(ps, axis=1))
        for i in range(2):
            r = 2 * q + i
            gr, gi = gv[:64, i * 128:(i + 1) * 128], gv[64:, i * 128:(i + 1) * 128]
            c, s = twi[r, 0], twi[r, 1]
            gc = jnp.concatenate([gr * c - gi * s, gi * c + gr * s], axis=1).astype(BF)
            o = dot_nt(mi[r], jnp.concatenate([gc, gc], axis=0))
            for ri in range(2):
                for k in range(2):
                    at = ri * 128 + k * 64
                    val = jnp.where(low, o[at:at + 32], o[at + 32:at + 64]).astype(BF)
                    for h in range(2):
                        osc[g, h, pl.ds(pl.multiple_of(ri * 512 + r * 16, 16), 16), pl.ds(k * 128, 128)] = (
                            val[h * 16:(h + 1) * 16])

    def inverse_step(g):
        def step(d, carry):
            q = lax.rem(me - d + SEQ_N, SEQ_N)
            pltpu.make_async_remote_copy(
                src_ref=hs.at[g, d], dst_ref=hr.at[g, q], send_sem=hs_sem.at[g, d],
                recv_sem=hr_sem.at[g, d], device_id=(me, mc), device_id_type=MESH).wait_recv()
            inverse_of(g, q)
            return carry
        return step

    def inverse_end(g):
        for h in range(2):
            back = dot(k0i[0], osc[g, h]) + dot(k0i[1], osc[g, h])
            y = dot((back * (1.0 / N)).astype(BF), permi[...]).astype(BF).reshape(16, 16, 256)
            for cl in range(2):
                cs[g, :, cl, pl.ds(h * 16, 16), :] = y[:, :, cl * 128:(cl + 1) * 128]
        sent = []
        for d in range(1, SEQ_N):
            copy = pltpu.make_async_remote_copy(
                src_ref=cs.at[g, peer[d]], dst_ref=cr.at[g, me], send_sem=cs_sem.at[g, d],
                recv_sem=cr_sem.at[g, d], device_id=(peer[d], mc), device_id_type=MESH)
            copy.start()
            sent.append(copy)
        cr[g, me] = cs[g, me]
        return sent

    def gating(g, arrivals):
        for copy in arrivals:
            copy.wait_recv()
        for cl in range(2):
            c32[cl] = cr[g, :, cl].reshape(512, 128).astype(F32)
        for cl in range(2):
            at = (2 * g + cl) * 16
            gain = gain_col[at:at + 16]
            for j in range(32):
                lanes = slice(j * 128, (j + 1) * 128)
                direct = c32[cl, pl.ds(j, 16, stride=32), :] + gain * sig[at:at + 16, lanes].astype(F32)
                gt[mc, g, pl.ds(cl * 16, 16), lanes] = (gate[at:at + 16, lanes].astype(F32) * direct).astype(BF)

    gathered = []
    every, first, second = pl.ds(0, 32), pl.ds(0, 16), pl.ds(16, 16)

    def pass_on(g, block, rows, to, n):
        copy = pltpu.make_async_remote_copy(
            src_ref=gt.at[block, g, rows], dst_ref=gt.at[block, g, rows], send_sem=gs_sem.at[g, n],
            recv_sem=gr_sem.at[g, n], device_id=(me, to), device_id_type=MESH)
        copy.start()
        gathered.append(copy)
        return copy

    def spread_own(g):
        return [pass_on(g, mc, every, pc, 0), pass_on(g, mc, every, upc, 1), pass_on(g, mc, every, dnc, 2)]

    def spread_partner(g, own):
        own[0].wait_recv()
        partner = [pass_on(g, pc, every, upc, 3), pass_on(g, pc, every, dnc, 4)]
        own[1].wait_recv()
        own[2].wait_recv()
        return partner + [pass_on(g, dnc, first, upc, 5), pass_on(g, upc, second, dnc, 6)]

    def spread_last(g, partner):
        partner[0].wait_recv()
        partner[1].wait_recv()
        return partner[2:] + [pass_on(g, flip(dnc), first, upc, 7), pass_on(g, flip(upc), second, dnc, 8)]

    inverse_of(0, me)
    lax.fori_loop(1, SEQ_N, inverse_step(0), 0)
    conv_a = inverse_end(0)
    inverse_of(1, me)
    lax.fori_loop(1, 9, inverse_step(1), 0)
    gating(0, conv_a)
    own_a = spread_own(0)
    lax.fori_loop(9, SEQ_N, inverse_step(1), 0)
    conv_b = inverse_end(1)
    partner_a = spread_partner(0, own_a)
    gating(1, conv_b)
    own_b = spread_own(1)
    last_a = spread_last(0, partner_a)
    partner_b = spread_partner(1, own_b)
    last_b = spread_last(1, partner_b)
    for copy in last_a + last_b:
        copy.wait_recv()
    for j in range(8):
        lanes = slice(j * 512, (j + 1) * 512)
        out_ref[:, lanes] = dot(w_ref[...], gt[:, :, :, lanes].reshape(512, 512)).astype(BF)
    for copy in x_out + h_out + conv_a + conv_b + gathered:
        copy.wait_send()


def body(signal, gate, spec_real, spec_imag, skip_gain, mix_weight):
    consts = [jnp.asarray(v) for v in constants()]
    rows = lambda v: v.reshape(64, 2, 32, 128).transpose(0, 2, 1, 3).reshape(4096, 128)
    anywhere = pl.BlockSpec(memory_space=pl.ANY)
    vmem = pl.BlockSpec(memory_space=pltpu.VMEM)
    buf = lambda *shape: pltpu.VMEM(shape, BF)
    wide = lambda *shape: pltpu.VMEM(shape, F32)
    dma = lambda *shape: pltpu.SemaphoreType.DMA(shape)
    held = [pltpu.VMEM(v.shape, v.dtype) for v in consts]
    return pl.pallas_call(
        kernel,
        out_shape=jax.ShapeDtypeStruct((64, 4096), BF),
        in_specs=[anywhere] * 4 + [vmem] * 2 + [anywhere] * len(consts),
        out_specs=vmem,
        scratch_shapes=[buf(64, 4096), buf(64, 4096), wide(2, 4096, 128)] + held + [
            wide(4, 512, 128), buf(16, 4, 32, 128), buf(16, 4, 32, 128),
            buf(2, 16, 2, 2, 64, 128), buf(2, 16, 2, 2, 64, 128), buf(32, 256, 128), wide(32, 256, 128),
            buf(2, 2, 1024, 256), buf(2, 16, 2, 32, 128), buf(2, 16, 2, 32, 128), wide(2, 512, 128),
            buf(CHAN_N, 2, 32, 4096),
            dma(14), dma(16), dma(16), dma(2, 16), dma(2, 16), dma(2, 16), dma(2, 16), dma(2, 9), dma(2, 9)],
        compiler_params=pltpu.CompilerParams(
            collective_id=0, has_side_effects=True, vmem_limit_bytes=60 * 1024 * 1024),
        cost_estimate=pl.CostEstimate(flops=10**10, bytes_accessed=3 * 10**7, transcendentals=0),
    )(signal, gate, rows(spec_real), rows(spec_imag), skip_gain.reshape(1, 64), mix_weight, *consts)


def solution(mesh):
    placed = (
        P("chan", "seq"),
        P("chan", "seq"),
        P("chan", "seq", None),
        P("chan", "seq", None),
        P("chan"),
        P("chan", None),
    )
    return jax.shard_map(
        body, mesh=mesh, in_specs=placed, out_specs=P("chan", "seq"), check_vma=False
    )
```

```python
import jax
import jax.numpy as jnp
import numpy as np
from jax import lax
from jax.experimental import pallas as pl
from jax.experimental.pallas import tpu as pltpu
from jax.sharding import PartitionSpec as P

BF = jnp.bfloat16
F32 = jnp.float32
N = 131072
SEQ_N = 16
CHAN_N = 8
CHUNKS = (1, 4)
SPLIT = 9
MESH = pl.DeviceIdType.MESH


def unit(numer, period):
    angle = 2.0 * np.pi * (np.asarray(numer, np.int64) % period) / period
    return np.cos(angle), np.sin(angle)


def tables():
    r = np.arange(32)
    a = np.arange(16)
    i, h, jb = np.meshgrid(np.arange(4), np.arange(2), np.arange(16), indexing="ij")
    s1 = (4 * (16 * h + jb) + i).reshape(-1)
    m2 = np.arange(128)
    m1 = np.arange(32)
    s2 = np.arange(32)
    eye16 = np.eye(16)
    eye4 = np.eye(4)
    c, s = unit(r[:, None] * a[None, :], 32)
    k0 = np.concatenate([np.kron(c, eye16), np.kron(-s, eye16)], 0)
    k0i = np.concatenate([np.kron(c.T, eye16), np.kron(-s.T, eye16)], 1)
    klow = 32 * m2[None, :] + r[:, None]
    c, s = unit(klow[:, :, None] * s1[None, None, :], 4096)
    m = np.concatenate([np.concatenate([c, s], 2), np.concatenate([-s, c], 2)], 1)
    mi = np.swapaxes(m, 1, 2)
    c, s = unit(klow[:, :, None] * np.tile(s2, 4)[None, None, :], N)
    tw = np.stack([c, s], 1)
    twi = np.swapaxes(tw, 2, 3)[:, :, :64]
    c, s = unit(m1[:, None] * s2[None, :], 32)
    c, s = np.kron(eye4, c), np.kron(eye4, s)
    l2 = np.concatenate([np.concatenate([c, s], 1), np.concatenate([-s, c], 1)], 0)
    c, s = unit(s2[:, None] * m1[None, :], 32)
    c, s = np.kron(np.eye(2), c), np.kron(np.eye(2), s)
    l2i = np.concatenate([np.concatenate([c, -s], 1), np.concatenate([s, c], 1)], 0)
    perm = np.zeros((4, 4, 32, 4, 4, 32))
    for ci in range(4):
        for ii in range(4):
            perm[ci, ii, np.arange(32), ii, ci, np.arange(32)] = 1
    perm = perm.reshape(512, 512)
    permi = np.zeros((4, 2, 32, 2, 4, 32))
    for ci in range(2):
        for ii in range(4):
            permi[ii, ci, np.arange(32), ci, ii, np.arange(32)] = 1
    permi = permi.reshape(256, 256)
    return k0, k0i, m, mi, tw, twi, l2, l2i, perm, permi


def split(x):
    x = np.asarray(x, np.float32)
    hi = x.astype(jnp.bfloat16)
    lo = (x - hi.astype(np.float32)).astype(jnp.bfloat16)
    return hi, lo


def constants():
    k0, k0i, m, mi, tw, twi, l2, l2i, perm, permi = tables()
    pair = lambda v: np.stack(split(v))
    one = lambda v: np.asarray(v, np.float32).astype(jnp.bfloat16)
    f = lambda v: np.asarray(v, np.float32)
    return [pair(k0), pair(k0i), one(m), one(mi), f(tw), f(twi), one(l2), one(l2i), one(perm), one(permi)]


def dot(a, b):
    return lax.dot_general(a, b, (((1,), (0,)), ((), ())), preferred_element_type=F32)


def dot_nt(a, b):
    return lax.dot_general(a, b, (((1,), (1,)), ((), ())), preferred_element_type=F32)


def kernel(sig_hbm, gate_hbm, hre_hbm, him_hbm, gain_ref, w_ref,
           k0_hbm, k0i_hbm, m_hbm, mi_hbm, tw_hbm, twi_hbm, l2_hbm, l2i_hbm, perm_hbm, permi_hbm,
           out_ref,
           sig, gate, h32, k0, k0i, m, mi, tw, twi, l2, l2i, perm, permi,
           s32, sx, xr, hs, hr, dsc, fsc, osc, cs, cr, c32, gt, wp, acc, ps, pr,
           load_sem, xs_sem, xr_sem, hs_sem, hr_sem, cs_sem, cr_sem, gs_sem, gr_sem, ps_sem, pr_sem):
    me = lax.axis_index("seq")
    mc = lax.axis_index("chan")
    peer = [lax.rem(me + d, SEQ_N) for d in range(SEQ_N)]
    source = [lax.rem(me - d + SEQ_N, SEQ_N) for d in range(SEQ_N)]
    xh, mz = lax.rem(mc, 2), lax.div(mc, 2)
    pc = mc + 1 - 2 * xh
    upc, dnc = lax.rem(mc + 2, CHAN_N), lax.rem(mc + 6, CHAN_N)

    barrier = pltpu.get_barrier_semaphore()
    for d in range(1, SEQ_N):
        pl.semaphore_signal(barrier, inc=1, device_id=(peer[d], mc), device_id_type=MESH)
    for c in (pc, upc, dnc):
        pl.semaphore_signal(barrier, inc=1, device_id=(me, c), device_id_type=MESH)

    pairs = [(sig_hbm, sig), (hre_hbm, h32.at[0]), (him_hbm, h32.at[1]), (perm_hbm, perm), (k0_hbm, k0),
             (m_hbm, m), (l2_hbm, l2), (tw_hbm, tw), (l2i_hbm, l2i), (twi_hbm, twi), (mi_hbm, mi),
             (k0i_hbm, k0i), (permi_hbm, permi), (gate_hbm, gate)]
    loads = [pltpu.make_async_copy(a, b, load_sem.at[n]) for n, (a, b) in enumerate(pairs)]
    for copy in loads:
        copy.start()

    square = lax.broadcasted_iota(jnp.int32, (64, 64), 0) == lax.broadcasted_iota(jnp.int32, (64, 64), 1)
    gain_col = jnp.sum(jnp.where(square, gain_ref[...], 0.0), axis=1, keepdims=True)

    loads[0].wait()
    for c in range(4):
        for j in range(32):
            s32[c, pl.ds(j, 16, stride=32), :] = sig[c * 16:(c + 1) * 16, j * 128:(j + 1) * 128].astype(F32)
    for c in range(4):
        sx[:, c] = s32[c].astype(BF).reshape(16, 32, 128)
    pl.semaphore_wait(barrier, SEQ_N + 2)
    x_out = []
    for d in range(1, SEQ_N):
        copy = pltpu.make_async_remote_copy(
            src_ref=sx.at[peer[d]], dst_ref=xr.at[me], send_sem=xs_sem.at[d], recv_sem=xr_sem.at[d],
            device_id=(peer[d], mc), device_id_type=MESH)
        copy.start()
        x_out.append(copy)
    xr[me] = sx[me]
    w_copy = pltpu.make_async_remote_copy(
        src_ref=w_ref, dst_ref=wp, send_sem=ps_sem.at[4], recv_sem=pr_sem.at[4],
        device_id=(me, pc), device_id_type=MESH)
    w_copy.start()

    loads[1].wait()
    loads[2].wait()

    def filter_copy(g, d):
        return pltpu.make_async_remote_copy(
            src_ref=hs.at[g, d], dst_ref=hr.at[g, me], send_sem=hs_sem.at[g, d],
            recv_sem=hr_sem.at[g, d], device_id=(peer[d], mc), device_id_type=MESH)

    def start_filter(g):
        for d in range(1, SEQ_N):
            filter_copy(g, d).start()

    def filter_sent(g):
        for d in range(1, SEQ_N):
            filter_copy(g, d).wait_send()

    for g in range(2):
        for d in list(range(1, SEQ_N)) + [0]:
            for part in range(2):
                for i in range(2):
                    for cl in range(2):
                        row = pl.multiple_of(((2 * g + cl) * 16 + peer[d]) * 64, 64) + i
                        val = h32[part, pl.ds(row, 32, stride=2), :].astype(BF)
                        if d == 0:
                            hr[g, me, part, i, pl.ds(cl * 32, 32), :] = val
                        else:
                            hs[g, d, part, i, pl.ds(cl * 32, 32), :] = val
        if g == 0:
            for copy in x_out:
                copy.wait_send()
            start_filter(0)

    for n in range(3, 8):
        loads[n].wait()
    for copy in x_out:
        copy.wait_recv()
    xa = jnp.concatenate([xr[:, c].reshape(512, 128) for c in range(4)], axis=1)
    spread = dot(xa, perm[...]).astype(BF).reshape(16, 32, 512)
    for h in range(2):
        rows = spread[:, h * 16:(h + 1) * 16].reshape(256, 512)
        dv = (dot(k0[0], rows) + dot(k0[1], rows)).astype(BF)
        for ri in range(2):
            for i in range(4):
                dsc[:, pl.ds(ri * 128 + i * 32 + h * 16, 16), :] = dv[
                    ri * 512:(ri + 1) * 512, i * 128:(i + 1) * 128].reshape(32, 16, 128)

    def forward(t, carry):
        ecs = []
        for u in range(4):
            r = t * 4 + u
            e = dot(m[r], dsc[r])
            er, ei = e[:128], e[128:]
            c, s = tw[r, 0], tw[r, 1]
            ecs.append(jnp.concatenate([er * c + ei * s, ei * c - er * s], axis=1).astype(BF))
        for u in range(0, 4, 2):
            f = dot_nt(l2[...], jnp.concatenate(ecs[u:u + 2], axis=0))
            fsc[t * 4 + u] = f[:, :128]
            fsc[t * 4 + u + 1] = f[:, 128:]
        return carry

    lax.fori_loop(0, 8, forward, 0)
    for n in range(8, 14):
        loads[n].wait()
    low = lax.broadcasted_iota(jnp.int32, (32, 128), 1) < 64

    def inverse_of(g, q):
        ps = []
        for i in range(2):
            r = 2 * q + i
            fr = fsc[r, pl.ds(g * 64, 64), :]
            fi = fsc[r, pl.ds(128 + g * 64, 64), :]
            re, im = hr[g, q, 0, i].astype(F32), hr[g, q, 1, i].astype(F32)
            ps.append(jnp.concatenate([fr * re - fi * im, fr * im + fi * re], axis=0).astype(BF))
        gv = dot(l2i[...], jnp.concatenate(ps, axis=1))
        for i in range(2):
            r = 2 * q + i
            gr, gi = gv[:64, i * 128:(i + 1) * 128], gv[64:, i * 128:(i + 1) * 128]
            c, s = twi[r, 0], twi[r, 1]
            gc = jnp.concatenate([gr * c - gi * s, gi * c + gr * s], axis=1).astype(BF)
            o = dot_nt(mi[r], jnp.concatenate([gc, gc], axis=0))
            for ri in range(2):
                for k in range(2):
                    at = ri * 128 + k * 64
                    val = jnp.where(low, o[at:at + 32], o[at + 32:at + 64]).astype(BF)
                    for h in range(2):
                        osc[g, h, pl.ds(pl.multiple_of(ri * 512 + r * 16, 16), 16), pl.ds(k * 128, 128)] = (
                            val[h * 16:(h + 1) * 16])

    def inverse_step(g):
        def step(d, carry):
            q = lax.rem(me - d + SEQ_N, SEQ_N)
            pltpu.make_async_remote_copy(
                src_ref=hs.at[g, d], dst_ref=hr.at[g, q], send_sem=hs_sem.at[g, d],
                recv_sem=hr_sem.at[g, d], device_id=(me, mc), device_id_type=MESH).wait_recv()
            inverse_of(g, q)
            return carry
        return step

    def inverse_end(g):
        for h in range(2):
            back = dot(k0i[0], osc[g, h]) + dot(k0i[1], osc[g, h])
            y = dot((back * (1.0 / N)).astype(BF), permi[...]).astype(BF).reshape(16, 16, 256)
            for cl in range(2):
                cs[g, :, cl, pl.ds(h * 16, 16), :] = y[:, :, cl * 128:(cl + 1) * 128]
        sent = []
        for d in range(1, SEQ_N):
            copy = pltpu.make_async_remote_copy(
                src_ref=cs.at[g, peer[d]], dst_ref=cr.at[g, me], send_sem=cs_sem.at[g, d],
                recv_sem=cr_sem.at[g, d], device_id=(peer[d], mc), device_id_type=MESH)
            copy.start()
            sent.append(copy)
        cr[g, me] = cs[g, me]
        return sent

    def gating(g, arrivals):
        for copy in arrivals:
            copy.wait_recv()
        for cl in range(2):
            c32[cl] = cr[g, :, cl].reshape(512, 128).astype(F32)
        width = 4096 // CHUNKS[g]
        for t in range(CHUNKS[g]):
            for cl in range(2):
                at = (2 * g + cl) * 16
                gain = gain_col[at:at + 16]
                for j in range(t * width // 128, (t + 1) * width // 128):
                    lanes = slice(j * 128, (j + 1) * 128)
                    direct = c32[cl, pl.ds(j, 16, stride=32), :] + gain * sig[at:at + 16, lanes].astype(F32)
                    gt[mz, g, pl.ds(cl * 16, 16), lanes] = (gate[at:at + 16, lanes].astype(F32) * direct).astype(BF)
            own[g, t] = [pass_on(g, t, mz, every, upc, 0), pass_on(g, t, mz, every, dnc, 1)]

    own, halves, gathered = {}, {}, []
    every, first, second = pl.ds(0, 32), pl.ds(0, 16), pl.ds(16, 16)
    zdn, zup = lax.rem(mz + 3, 4), lax.rem(mz + 1, 4)

    def pass_on(g, t, block, rows, to, n):
        width = 4096 // CHUNKS[g]
        part = gt.at[block, g, rows, pl.ds(t * width, width)]
        copy = pltpu.make_async_remote_copy(
            src_ref=part, dst_ref=part, send_sem=gs_sem.at[g, t * 4 + n],
            recv_sem=gr_sem.at[g, t * 4 + n], device_id=(me, to), device_id_type=MESH)
        copy.start()
        gathered.append(copy)
        return copy

    def send_on(g):
        for t in range(CHUNKS[g]):
            own[g, t][0].wait_recv()
            own[g, t][1].wait_recv()
            halves[g, t] = [pass_on(g, t, zdn, first, upc, 2), pass_on(g, t, zup, second, dnc, 3)]

    at_k = lax.broadcasted_iota(jnp.int32, (512, 128), 0)
    at_n = lax.broadcasted_iota(jnp.int32, (512, 128), 1)

    def weights(g):
        pick = at_k == (at_n // 32) * 128 + xh * 64 + g * 32 + at_n % 32
        both = jnp.concatenate([w_ref[...], wp[...]], axis=0)
        return dot(both, jnp.where(pick, 1.0, 0.0).astype(BF)).astype(BF)

    def partial(g, wg, lanes):
        return dot(wg, gt[:, g, :, lanes].reshape(128, lanes.stop - lanes.start))

    filter_sent(0)
    start_filter(1)
    inverse_of(0, me)
    lax.fori_loop(1, SEQ_N, inverse_step(0), 0)
    conv_a = inverse_end(0)
    inverse_of(1, me)
    lax.fori_loop(1, SPLIT, inverse_step(1), 0)
    gating(0, conv_a)
    lax.fori_loop(SPLIT, SEQ_N, inverse_step(1), 0)
    conv_b = inverse_end(1)
    send_on(0)
    w_copy.wait_recv()
    w0, w1 = weights(0), weights(1)
    gating(1, conv_b)
    for copy in halves[0, 0]:
        copy.wait_recv()
    for j in range(8):
        lanes = slice(j * 512, (j + 1) * 512)
        acc[:, lanes] = partial(0, w0, lanes)
    send_on(1)
    swaps = []
    width = 4096 // CHUNKS[1]
    for t in range(CHUNKS[1]):
        for copy in halves[1, t]:
            copy.wait_recv()
        lanes = slice(t * width, (t + 1) * width)
        full = acc[:, lanes] + partial(1, w1, lanes)
        acc[0:64, lanes] = full[:64]
        ps[:, lanes] = full[64:].astype(BF)
        part = pl.ds(t * width, width)
        copy = pltpu.make_async_remote_copy(
            src_ref=ps.at[:, part], dst_ref=pr.at[:, part], send_sem=ps_sem.at[t], recv_sem=pr_sem.at[t],
            device_id=(me, pc), device_id_type=MESH)
        copy.start()
        swaps.append(copy)
    for t, copy in enumerate(swaps):
        copy.wait_recv()
        lanes = slice(t * width, (t + 1) * width)
        out_ref[:, lanes] = (acc[0:64, lanes] + pr[:, lanes].astype(F32)).astype(BF)
    filter_sent(1)
    for copy in conv_a + conv_b + gathered + swaps + [w_copy]:
        copy.wait_send()


def body(signal, gate, spec_real, spec_imag, skip_gain, mix_weight):
    consts = [jnp.asarray(v) for v in constants()]
    rows = lambda v: v.reshape(64, 2, 32, 128).transpose(0, 2, 1, 3).reshape(4096, 128)
    anywhere = pl.BlockSpec(memory_space=pl.ANY)
    vmem = pl.BlockSpec(memory_space=pltpu.VMEM)
    buf = lambda *shape: pltpu.VMEM(shape, BF)
    wide = lambda *shape: pltpu.VMEM(shape, F32)
    dma = lambda *shape: pltpu.SemaphoreType.DMA(shape)
    held = [pltpu.VMEM(v.shape, v.dtype) for v in consts]
    return pl.pallas_call(
        kernel,
        out_shape=jax.ShapeDtypeStruct((64, 4096), BF),
        in_specs=[anywhere] * 4 + [vmem] * 2 + [anywhere] * len(consts),
        out_specs=vmem,
        scratch_shapes=[buf(64, 4096), buf(64, 4096), wide(2, 4096, 128)] + held + [
            wide(4, 512, 128), buf(16, 4, 32, 128), buf(16, 4, 32, 128),
            buf(2, 16, 2, 2, 64, 128), buf(2, 16, 2, 2, 64, 128), buf(32, 256, 128), wide(32, 256, 128),
            buf(2, 2, 1024, 256), buf(2, 16, 2, 32, 128), buf(2, 16, 2, 32, 128), wide(2, 512, 128),
            buf(4, 2, 32, 4096), buf(64, 512), wide(128, 4096), buf(64, 4096), buf(64, 4096),
            dma(14), dma(16), dma(16), dma(2, 16), dma(2, 16), dma(2, 16), dma(2, 16), dma(2, 16), dma(2, 16), dma(5), dma(5)],
        compiler_params=pltpu.CompilerParams(
            collective_id=0, has_side_effects=True, vmem_limit_bytes=60 * 1024 * 1024),
        cost_estimate=pl.CostEstimate(flops=10**10, bytes_accessed=3 * 10**7, transcendentals=0),
    )(signal, gate, rows(spec_real), rows(spec_imag), skip_gain.reshape(1, 64), mix_weight, *consts)


def solution(mesh):
    placed = (
        P("chan", "seq"),
        P("chan", "seq"),
        P("chan", "seq", None),
        P("chan", "seq", None),
        P("chan"),
        P("chan", None),
    )
    return jax.shard_map(
        body, mesh=mesh, in_specs=placed, out_specs=P("chan", "seq"), check_vma=False
    )
```

```python
import jax
import jax.numpy as jnp
import numpy as np
from jax import lax
from jax.experimental import pallas as pl
from jax.experimental.pallas import tpu as pltpu
from jax.sharding import PartitionSpec as P

BF = jnp.bfloat16
F32 = jnp.float32
N = 131072
SEQ_N = 16
CHAN_N = 8
CHUNKS = (1, 4)
SPLIT = 4
MESH = pl.DeviceIdType.MESH


def unit(numer, period):
    angle = 2.0 * np.pi * (np.asarray(numer, np.int64) % period) / period
    return np.cos(angle), np.sin(angle)


def tables():
    r = np.arange(32)
    a = np.arange(16)
    i, h, jb = np.meshgrid(np.arange(4), np.arange(2), np.arange(16), indexing="ij")
    s1 = (4 * (16 * h + jb) + i).reshape(-1)
    m2 = np.arange(128)
    m1 = np.arange(32)
    s2 = np.arange(32)
    eye16 = np.eye(16)
    eye4 = np.eye(4)
    c, s = unit(r[:, None] * a[None, :], 32)
    k0 = np.concatenate([np.kron(c, eye16), np.kron(-s, eye16)], 0)
    k0i = np.concatenate([np.kron(c.T, eye16), np.kron(-s.T, eye16)], 1)
    klow = 32 * m2[None, :] + r[:, None]
    c, s = unit(klow[:, :, None] * s1[None, None, :], 4096)
    m = np.concatenate([np.concatenate([c, s], 2), np.concatenate([-s, c], 2)], 1)
    mi = np.swapaxes(m, 1, 2)
    c, s = unit(klow[:, :, None] * np.tile(s2, 4)[None, None, :], N)
    tw = np.stack([c, s], 1)
    twi = np.swapaxes(tw, 2, 3)[:, :, :64]
    c, s = unit(m1[:, None] * s2[None, :], 32)
    c, s = np.kron(eye4, c), np.kron(eye4, s)
    l2 = np.concatenate([np.concatenate([c, s], 1), np.concatenate([-s, c], 1)], 0)
    c, s = unit(s2[:, None] * m1[None, :], 32)
    c, s = np.kron(np.eye(2), c), np.kron(np.eye(2), s)
    l2i = np.concatenate([np.concatenate([c, -s], 1), np.concatenate([s, c], 1)], 0)
    perm = np.zeros((4, 4, 32, 4, 4, 32))
    for ci in range(4):
        for ii in range(4):
            perm[ci, ii, np.arange(32), ii, ci, np.arange(32)] = 1
    perm = perm.reshape(512, 512)
    permi = np.zeros((4, 2, 32, 2, 4, 32))
    for ci in range(2):
        for ii in range(4):
            permi[ii, ci, np.arange(32), ci, ii, np.arange(32)] = 1
    permi = permi.reshape(256, 256)
    return k0, k0i, m, mi, tw, twi, l2, l2i, perm, permi


def split(x):
    x = np.asarray(x, np.float32)
    hi = x.astype(jnp.bfloat16)
    lo = (x - hi.astype(np.float32)).astype(jnp.bfloat16)
    return hi, lo


def constants():
    k0, k0i, m, mi, tw, twi, l2, l2i, perm, permi = tables()
    pair = lambda v: np.stack(split(v))
    one = lambda v: np.asarray(v, np.float32).astype(jnp.bfloat16)
    f = lambda v: np.asarray(v, np.float32)
    return [pair(k0), pair(k0i), one(m), one(mi), f(tw), f(twi), one(l2), one(l2i), one(perm), one(permi)]


def dot(a, b):
    return lax.dot_general(a, b, (((1,), (0,)), ((), ())), preferred_element_type=F32)


def dot_nt(a, b):
    return lax.dot_general(a, b, (((1,), (1,)), ((), ())), preferred_element_type=F32)


def kernel(sig_hbm, gate_hbm, hre_hbm, him_hbm, gain_ref, w_hbm,
           k0_hbm, k0i_hbm, m_hbm, mi_hbm, tw_hbm, twi_hbm, l2_hbm, l2i_hbm, perm_hbm, permi_hbm,
           out_hbm,
           w_ref, out_ref, sig, gate, h32, k0, k0i, m, mi, tw, twi, l2, l2i, perm, permi,
           s32, sx, xr, hs, hr, dsc, fsc, osc, cs, cr, c32, gt, wp, acc, ps, pr,
           load_sem, xs_sem, xr_sem, hs_sem, hr_sem, cs_sem, cr_sem, gs_sem, gr_sem, ps_sem, pr_sem, out_sem):
    me = lax.axis_index("seq")
    mc = lax.axis_index("chan")
    peer = [lax.rem(me + d, SEQ_N) for d in range(SEQ_N)]
    source = [lax.rem(me - d + SEQ_N, SEQ_N) for d in range(SEQ_N)]
    xh, mz = lax.rem(mc, 2), lax.div(mc, 2)
    pc = mc + 1 - 2 * xh
    upc, dnc = lax.rem(mc + 2, CHAN_N), lax.rem(mc + 6, CHAN_N)

    barrier = pltpu.get_barrier_semaphore()
    for d in range(1, SEQ_N):
        pl.semaphore_signal(barrier, inc=1, device_id=(peer[d], mc), device_id_type=MESH)
    for c in (pc, upc, dnc):
        pl.semaphore_signal(barrier, inc=1, device_id=(me, c), device_id_type=MESH)

    pairs = [(sig_hbm, sig), (hre_hbm, h32.at[0]), (him_hbm, h32.at[1]), (perm_hbm, perm), (k0_hbm, k0),
             (m_hbm, m), (l2_hbm, l2), (tw_hbm, tw), (l2i_hbm, l2i), (twi_hbm, twi), (mi_hbm, mi),
             (k0i_hbm, k0i), (permi_hbm, permi), (gate_hbm, gate), (w_hbm, w_ref)]
    loads = [pltpu.make_async_copy(a, b, load_sem.at[n]) for n, (a, b) in enumerate(pairs)]
    for copy in loads:
        copy.start()

    square = lax.broadcasted_iota(jnp.int32, (64, 64), 0) == lax.broadcasted_iota(jnp.int32, (64, 64), 1)
    gain_col = jnp.sum(jnp.where(square, gain_ref[...], 0.0), axis=1, keepdims=True)

    loads[0].wait()
    for c in range(4):
        for j in range(32):
            s32[c, pl.ds(j, 16, stride=32), :] = sig[c * 16:(c + 1) * 16, j * 128:(j + 1) * 128].astype(F32)
    for c in range(4):
        sx[:, c] = s32[c].astype(BF).reshape(16, 32, 128)
    pl.semaphore_wait(barrier, SEQ_N + 2)
    x_out = []
    for d in range(1, SEQ_N):
        copy = pltpu.make_async_remote_copy(
            src_ref=sx.at[peer[d]], dst_ref=xr.at[me], send_sem=xs_sem.at[d], recv_sem=xr_sem.at[d],
            device_id=(peer[d], mc), device_id_type=MESH)
        copy.start()
        x_out.append(copy)
    xr[me] = sx[me]
    loads[14].wait()
    w_copy = pltpu.make_async_remote_copy(
        src_ref=w_ref, dst_ref=wp, send_sem=ps_sem.at[4], recv_sem=pr_sem.at[4],
        device_id=(me, pc), device_id_type=MESH)
    w_copy.start()

    loads[1].wait()
    loads[2].wait()

    def filter_copy(g, d):
        return pltpu.make_async_remote_copy(
            src_ref=hs.at[g, d], dst_ref=hr.at[g, me], send_sem=hs_sem.at[g, d],
            recv_sem=hr_sem.at[g, d], device_id=(peer[d], mc), device_id_type=MESH)

    def start_filter(g):
        for d in range(1, SEQ_N):
            filter_copy(g, d).start()

    def filter_sent(g):
        for d in range(1, SEQ_N):
            filter_copy(g, d).wait_send()

    for g in range(2):
        for d in list(range(1, SEQ_N)) + [0]:
            for part in range(2):
                for i in range(2):
                    for cl in range(2):
                        row = pl.multiple_of(((2 * g + cl) * 16 + peer[d]) * 64, 64) + i
                        val = h32[part, pl.ds(row, 32, stride=2), :].astype(BF)
                        if d == 0:
                            hr[g, me, part, i, pl.ds(cl * 32, 32), :] = val
                        else:
                            hs[g, d, part, i, pl.ds(cl * 32, 32), :] = val
        if g == 0:
            for copy in x_out:
                copy.wait_send()
            start_filter(0)

    for n in range(3, 8):
        loads[n].wait()
    for copy in x_out:
        copy.wait_recv()
    xa = jnp.concatenate([xr[:, c].reshape(512, 128) for c in range(4)], axis=1)
    spread = dot(xa, perm[...]).astype(BF).reshape(16, 32, 512)
    for h in range(2):
        rows = spread[:, h * 16:(h + 1) * 16].reshape(256, 512)
        dv = (dot(k0[0], rows) + dot(k0[1], rows)).astype(BF)
        for ri in range(2):
            for i in range(4):
                dsc[:, pl.ds(ri * 128 + i * 32 + h * 16, 16), :] = dv[
                    ri * 512:(ri + 1) * 512, i * 128:(i + 1) * 128].reshape(32, 16, 128)

    def forward(t, carry):
        ecs = []
        for u in range(4):
            r = t * 4 + u
            e = dot(m[r], dsc[r])
            er, ei = e[:128], e[128:]
            c, s = tw[r, 0], tw[r, 1]
            ecs.append(jnp.concatenate([er * c + ei * s, ei * c - er * s], axis=1).astype(BF))
        for u in range(0, 4, 2):
            f = dot_nt(l2[...], jnp.concatenate(ecs[u:u + 2], axis=0))
            fsc[t * 4 + u] = f[:, :128]
            fsc[t * 4 + u + 1] = f[:, 128:]
        return carry

    lax.fori_loop(0, 8, forward, 0)
    for n in range(8, 14):
        loads[n].wait()
    low = lax.broadcasted_iota(jnp.int32, (32, 128), 1) < 64

    def inverse_of(g, qs):
        rs = [2 * q + i for q in qs for i in range(2)]
        ps = []
        for n, r in enumerate(rs):
            fr = fsc[r, pl.ds(g * 64, 64), :]
            fi = fsc[r, pl.ds(128 + g * 64, 64), :]
            re, im = hr[g, qs[n // 2], 0, n % 2].astype(F32), hr[g, qs[n // 2], 1, n % 2].astype(F32)
            ps.append(jnp.concatenate([fr * re - fi * im, fr * im + fi * re], axis=0).astype(BF))
        gv = [dot(l2i[...], jnp.concatenate(ps[n:n + 2], axis=1)) for n in range(0, len(rs), 2)]
        os = []
        for n, r in enumerate(rs):
            half = gv[n // 2][:, (n % 2) * 128:(n % 2 + 1) * 128]
            gr, gi = half[:64], half[64:]
            c, s = twi[r, 0], twi[r, 1]
            gc = jnp.concatenate([gr * c - gi * s, gi * c + gr * s], axis=1).astype(BF)
            os.append(dot_nt(mi[r], jnp.concatenate([gc, gc], axis=0)))
        for r, o in zip(rs, os):
            for ri in range(2):
                for k in range(2):
                    at = ri * 128 + k * 64
                    val = jnp.where(low, o[at:at + 32], o[at + 32:at + 64]).astype(BF)
                    for h in range(2):
                        osc[g, h, pl.ds(pl.multiple_of(ri * 512 + r * 16, 16), 16), pl.ds(k * 128, 128)] = (
                            val[h * 16:(h + 1) * 16])

    def inverse_step(g):
        def step(t, carry):
            for u in range(2):
                d = 2 * t + u
                pltpu.make_async_remote_copy(
                    src_ref=hs.at[g, d], dst_ref=hr.at[g, lax.rem(me - d + SEQ_N, SEQ_N)],
                    send_sem=hs_sem.at[g, d], recv_sem=hr_sem.at[g, d], device_id=(me, mc),
                    device_id_type=MESH).wait_recv()
            inverse_of(g, [lax.rem(me - 2 * t - u + SEQ_N, SEQ_N) for u in range(2)])
            return carry
        return step

    def inverse_first(g):
        filter_copy(g, 1).wait_recv()
        inverse_of(g, [me, source[1]])

    def inverse_end(g):
        for h in range(2):
            back = dot(k0i[0], osc[g, h]) + dot(k0i[1], osc[g, h])
            y = dot((back * (1.0 / N)).astype(BF), permi[...]).astype(BF).reshape(16, 16, 256)
            for cl in range(2):
                cs[g, :, cl, pl.ds(h * 16, 16), :] = y[:, :, cl * 128:(cl + 1) * 128]
        sent = []
        for d in range(1, SEQ_N):
            copy = pltpu.make_async_remote_copy(
                src_ref=cs.at[g, peer[d]], dst_ref=cr.at[g, me], send_sem=cs_sem.at[g, d],
                recv_sem=cr_sem.at[g, d], device_id=(peer[d], mc), device_id_type=MESH)
            copy.start()
            sent.append(copy)
        cr[g, me] = cs[g, me]
        return sent

    own, gathered, done = {}, [], []

    def gating(g, arrivals):
        for copy in arrivals:
            copy.wait_recv()
        for cl in range(2):
            c32[cl] = cr[g, :, cl].reshape(512, 128).astype(F32)
        width = 4096 // CHUNKS[g]
        for t in range(CHUNKS[g]):
            for cl in range(2):
                at = (2 * g + cl) * 16
                gain = gain_col[at:at + 16]
                for j in range(t * width // 128, (t + 1) * width // 128):
                    lanes = slice(j * 128, (j + 1) * 128)
                    direct = c32[cl, pl.ds(j, 16, stride=32), :] + gain * sig[at:at + 16, lanes].astype(F32)
                    gt[mz, g, pl.ds(cl * 16, 16), lanes] = (gate[at:at + 16, lanes].astype(F32) * direct).astype(BF)
            own[g, t] = [pass_on(g, t, mz, every, upc, 0), pass_on(g, t, mz, every, dnc, 1)]

    halves = {}
    every, first, second = pl.ds(0, 32), pl.ds(0, 16), pl.ds(16, 16)
    zdn, zup = lax.rem(mz + 3, 4), lax.rem(mz + 1, 4)

    def pass_on(g, t, block, rows, to, n):
        width = 4096 // CHUNKS[g]
        part = gt.at[block, g, rows, pl.ds(t * width, width)]
        copy = pltpu.make_async_remote_copy(
            src_ref=part, dst_ref=part, send_sem=gs_sem.at[g, t * 4 + n],
            recv_sem=gr_sem.at[g, t * 4 + n], device_id=(me, to), device_id_type=MESH)
        copy.start()
        gathered.append(copy)
        return copy

    def send_on(g, chunks):
        for t in chunks:
            own[g, t][0].wait_recv()
            own[g, t][1].wait_recv()
            halves[g, t] = [pass_on(g, t, zdn, first, upc, 2), pass_on(g, t, zup, second, dnc, 3)]

    at_k = lax.broadcasted_iota(jnp.int32, (512, 128), 0)
    at_n = lax.broadcasted_iota(jnp.int32, (512, 128), 1)

    def weights(g):
        pick = at_k == (at_n // 32) * 128 + xh * 64 + g * 32 + at_n % 32
        both = jnp.concatenate([w_ref[...], wp[...]], axis=0)
        return dot(both, jnp.where(pick, 1.0, 0.0).astype(BF)).astype(BF)

    def partial(g, wg, lanes):
        return dot(wg, gt[:, g, :, lanes].reshape(128, lanes.stop - lanes.start))

    filter_sent(0)
    start_filter(1)
    inverse_first(0)
    lax.fori_loop(1, 8, inverse_step(0), 0)
    conv_a = inverse_end(0)
    inverse_first(1)
    lax.fori_loop(1, SPLIT, inverse_step(1), 0)
    gating(0, conv_a)
    lax.fori_loop(SPLIT, 8, inverse_step(1), 0)
    conv_b = inverse_end(1)
    send_on(0, [0])
    w_copy.wait_recv()
    w0, w1 = weights(0), weights(1)
    gating(1, conv_b)
    for copy in halves[0, 0]:
        copy.wait_recv()
    for j in range(8):
        lanes = slice(j * 512, (j + 1) * 512)
        acc[:, lanes] = partial(0, w0, lanes)
    swaps = []
    send_on(1, [0])
    width = 4096 // CHUNKS[1]
    for t in range(CHUNKS[1]):
        if t + 1 < CHUNKS[1]:
            send_on(1, [t + 1])
        for copy in halves[1, t]:
            copy.wait_recv()
        lanes = slice(t * width, (t + 1) * width)
        full = acc[:, lanes] + partial(1, w1, lanes)
        acc[0:64, lanes] = full[:64]
        ps[:, lanes] = full[64:].astype(BF)
        part = pl.ds(t * width, width)
        copy = pltpu.make_async_remote_copy(
            src_ref=ps.at[:, part], dst_ref=pr.at[:, part], send_sem=ps_sem.at[t], recv_sem=pr_sem.at[t],
            device_id=(me, pc), device_id_type=MESH)
        copy.start()
        swaps.append(copy)
    stores = []
    for t, copy in enumerate(swaps):
        copy.wait_recv()
        lanes = slice(t * width, (t + 1) * width)
        out_ref[:, lanes] = (acc[0:64, lanes] + pr[:, lanes].astype(F32)).astype(BF)
        copy = pltpu.make_async_copy(out_ref.at[:, lanes], out_hbm.at[:, lanes], out_sem.at[t])
        copy.start()
        stores.append(copy)
    for copy in stores:
        copy.wait()
    filter_sent(1)
    for copy in conv_a + conv_b + gathered + swaps + [w_copy]:
        if id(copy) not in done:
            copy.wait_send()


def body(signal, gate, spec_real, spec_imag, skip_gain, mix_weight):
    consts = [jnp.asarray(v) for v in constants()]
    rows = lambda v: v.reshape(64, 2, 32, 128).transpose(0, 2, 1, 3).reshape(4096, 128)
    anywhere = pl.BlockSpec(memory_space=pl.ANY)
    vmem = pl.BlockSpec(memory_space=pltpu.VMEM)
    buf = lambda *shape: pltpu.VMEM(shape, BF)
    wide = lambda *shape: pltpu.VMEM(shape, F32)
    dma = lambda *shape: pltpu.SemaphoreType.DMA(shape)
    held = [pltpu.VMEM(v.shape, v.dtype) for v in consts]
    return pl.pallas_call(
        kernel,
        out_shape=jax.ShapeDtypeStruct((64, 4096), BF),
        in_specs=[anywhere] * 4 + [vmem, anywhere] + [anywhere] * len(consts),
        out_specs=anywhere,
        scratch_shapes=[buf(64, 512), buf(64, 4096), buf(64, 4096), buf(64, 4096), wide(2, 4096, 128)] + held + [
            wide(4, 512, 128), buf(16, 4, 32, 128), buf(16, 4, 32, 128),
            buf(2, 16, 2, 2, 64, 128), buf(2, 16, 2, 2, 64, 128), buf(32, 256, 128), wide(32, 256, 128),
            buf(2, 2, 1024, 256), buf(2, 16, 2, 32, 128), buf(2, 16, 2, 32, 128), wide(2, 512, 128),
            buf(4, 2, 32, 4096), buf(64, 512), wide(128, 4096), buf(64, 4096), buf(64, 4096),
            dma(15), dma(16), dma(16), dma(2, 16), dma(2, 16), dma(2, 16), dma(2, 16), dma(2, 16), dma(2, 16), dma(5), dma(5), dma(4)],
        compiler_params=pltpu.CompilerParams(
            collective_id=0, has_side_effects=True, vmem_limit_bytes=60 * 1024 * 1024),
        cost_estimate=pl.CostEstimate(flops=10**10, bytes_accessed=3 * 10**7, transcendentals=0),
    )(signal, gate, rows(spec_real), rows(spec_imag), skip_gain.reshape(1, 64), mix_weight, *consts)


def solution(mesh):
    placed = (
        P("chan", "seq"),
        P("chan", "seq"),
        P("chan", "seq", None),
        P("chan", "seq", None),
        P("chan"),
        P("chan", None),
    )
    return jax.shard_map(
        body, mesh=mesh, in_specs=placed, out_specs=P("chan", "seq"), check_vma=False
    )
```

```python
import jax
import jax.numpy as jnp
import numpy as np
from jax import lax
from jax.experimental import pallas as pl
from jax.experimental.pallas import tpu as pltpu
from jax.sharding import PartitionSpec as P

BF = jnp.bfloat16
F32 = jnp.float32
N = 131072
SEQ_N = 16
CHAN_N = 8
CHUNKS = (2, 4)
SPLIT = 4
MESH = pl.DeviceIdType.MESH


def unit(numer, period):
    angle = 2.0 * np.pi * (np.asarray(numer, np.int64) % period) / period
    return np.cos(angle), np.sin(angle)


def tables():
    r = np.arange(32)
    a = np.arange(16)
    i, h, jb = np.meshgrid(np.arange(4), np.arange(2), np.arange(16), indexing="ij")
    s1 = (4 * (16 * h + jb) + i).reshape(-1)
    m2 = np.arange(128)
    m1 = np.arange(32)
    s2 = np.arange(32)
    eye16 = np.eye(16)
    eye4 = np.eye(4)
    c, s = unit(r[:, None] * a[None, :], 32)
    k0 = np.concatenate([np.kron(c, eye16), np.kron(-s, eye16)], 0)
    k0i = np.concatenate([np.kron(c.T, eye16), np.kron(-s.T, eye16)], 1)
    klow = 32 * m2[None, :] + r[:, None]
    c, s = unit(klow[:, :, None] * s1[None, None, :], 4096)
    m = np.concatenate([np.concatenate([c, s], 2), np.concatenate([-s, c], 2)], 1)
    mi = np.swapaxes(m, 1, 2)
    c, s = unit(klow[:, :, None] * np.tile(s2, 4)[None, None, :], N)
    tw = np.stack([c, s], 1)
    twi = np.swapaxes(tw, 2, 3)[:, :, :64]
    c, s = unit(m1[:, None] * s2[None, :], 32)
    c, s = np.kron(eye4, c), np.kron(eye4, s)
    l2 = np.concatenate([np.concatenate([c, s], 1), np.concatenate([-s, c], 1)], 0)
    c, s = unit(s2[:, None] * m1[None, :], 32)
    c, s = np.kron(np.eye(2), c), np.kron(np.eye(2), s)
    l2i = np.concatenate([np.concatenate([c, -s], 1), np.concatenate([s, c], 1)], 0)
    perm = np.zeros((4, 4, 32, 4, 4, 32))
    for ci in range(4):
        for ii in range(4):
            perm[ci, ii, np.arange(32), ii, ci, np.arange(32)] = 1
    perm = perm.reshape(512, 512)
    permi = np.zeros((4, 2, 32, 2, 4, 32))
    for ci in range(2):
        for ii in range(4):
            permi[ii, ci, np.arange(32), ci, ii, np.arange(32)] = 1
    permi = permi.reshape(256, 256)
    return k0, k0i, m, mi, tw, twi, l2, l2i, perm, permi


def split(x):
    x = np.asarray(x, np.float32)
    hi = x.astype(jnp.bfloat16)
    lo = (x - hi.astype(np.float32)).astype(jnp.bfloat16)
    return hi, lo


def constants():
    k0, k0i, m, mi, tw, twi, l2, l2i, perm, permi = tables()
    pair = lambda v: np.stack(split(v))
    one = lambda v: np.asarray(v, np.float32).astype(jnp.bfloat16)
    f = lambda v: np.asarray(v, np.float32)
    return [pair(k0), pair(k0i), one(m), one(mi), f(tw), f(twi), one(l2), one(l2i), one(perm), one(permi)]


def dot(a, b):
    return lax.dot_general(a, b, (((1,), (0,)), ((), ())), preferred_element_type=F32)


def dot_nt(a, b):
    return lax.dot_general(a, b, (((1,), (1,)), ((), ())), preferred_element_type=F32)


def kernel(sig_hbm, gate_hbm, hre_hbm, him_hbm, gain_ref, w_hbm,
           k0_hbm, k0i_hbm, m_hbm, mi_hbm, tw_hbm, twi_hbm, l2_hbm, l2i_hbm, perm_hbm, permi_hbm,
           out_hbm,
           w_ref, out_ref, sig, gate, h32, k0, k0i, m, mi, tw, twi, l2, l2i, perm, permi,
           s32, sx, xr, hs, hr, dsc, fsc, osc, cs, cr, c32, gt, wp, acc, ps, pr,
           load_sem, xs_sem, xr_sem, hs_sem, hr_sem, cs_sem, cr_sem, gs_sem, gr_sem, ps_sem, pr_sem, out_sem):
    me = lax.axis_index("seq")
    mc = lax.axis_index("chan")
    peer = [lax.rem(me + d, SEQ_N) for d in range(SEQ_N)]
    source = [lax.rem(me - d + SEQ_N, SEQ_N) for d in range(SEQ_N)]
    xh, mz = lax.rem(mc, 2), lax.div(mc, 2)
    pc = mc + 1 - 2 * xh
    upc, dnc = lax.rem(mc + 2, CHAN_N), lax.rem(mc + 6, CHAN_N)

    barrier = pltpu.get_barrier_semaphore()
    for d in range(1, SEQ_N):
        pl.semaphore_signal(barrier, inc=1, device_id=(peer[d], mc), device_id_type=MESH)
    for c in (pc, upc, dnc):
        pl.semaphore_signal(barrier, inc=1, device_id=(me, c), device_id_type=MESH)

    pairs = [(sig_hbm, sig), (hre_hbm, h32.at[0]), (him_hbm, h32.at[1]), (perm_hbm, perm), (k0_hbm, k0),
             (m_hbm, m), (l2_hbm, l2), (tw_hbm, tw), (l2i_hbm, l2i), (twi_hbm, twi), (mi_hbm, mi),
             (k0i_hbm, k0i), (permi_hbm, permi), (gate_hbm, gate), (w_hbm, w_ref)]
    loads = [pltpu.make_async_copy(a, b, load_sem.at[n]) for n, (a, b) in enumerate(pairs)]
    for copy in loads:
        copy.start()

    square = lax.broadcasted_iota(jnp.int32, (64, 64), 0) == lax.broadcasted_iota(jnp.int32, (64, 64), 1)
    gain_col = jnp.sum(jnp.where(square, gain_ref[...], 0.0), axis=1, keepdims=True)

    loads[0].wait()
    for c in range(4):
        for j in range(32):
            s32[c, pl.ds(j, 16, stride=32), :] = sig[c * 16:(c + 1) * 16, j * 128:(j + 1) * 128].astype(F32)
    for c in range(4):
        sx[:, c] = s32[c].astype(BF).reshape(16, 32, 128)
    pl.semaphore_wait(barrier, SEQ_N + 2)
    x_out = []
    for d in range(1, SEQ_N):
        copy = pltpu.make_async_remote_copy(
            src_ref=sx.at[peer[d]], dst_ref=xr.at[me], send_sem=xs_sem.at[d], recv_sem=xr_sem.at[d],
            device_id=(peer[d], mc), device_id_type=MESH)
        copy.start()
        x_out.append(copy)
    xr[me] = sx[me]
    loads[14].wait()
    w_copy = pltpu.make_async_remote_copy(
        src_ref=w_ref, dst_ref=wp, send_sem=ps_sem.at[4], recv_sem=pr_sem.at[4],
        device_id=(me, pc), device_id_type=MESH)
    w_copy.start()

    loads[1].wait()
    loads[2].wait()

    def filter_copy(g, d):
        return pltpu.make_async_remote_copy(
            src_ref=hs.at[g, d], dst_ref=hr.at[g, me], send_sem=hs_sem.at[g, d],
            recv_sem=hr_sem.at[g, d], device_id=(peer[d], mc), device_id_type=MESH)

    def start_filter(g):
        for d in range(1, SEQ_N):
            filter_copy(g, d).start()

    def filter_sent(g):
        for d in range(1, SEQ_N):
            filter_copy(g, d).wait_send()

    for g in range(2):
        for d in list(range(1, SEQ_N)) + [0]:
            for part in range(2):
                for i in range(2):
                    for cl in range(2):
                        row = pl.multiple_of(((2 * g + cl) * 16 + peer[d]) * 64, 64) + i
                        val = h32[part, pl.ds(row, 32, stride=2), :].astype(BF)
                        if d == 0:
                            hr[g, me, part, i, pl.ds(cl * 32, 32), :] = val
                        else:
                            hs[g, d, part, i, pl.ds(cl * 32, 32), :] = val
        if g == 0:
            for copy in x_out:
                copy.wait_send()
            start_filter(0)

    for n in range(3, 8):
        loads[n].wait()
    for copy in x_out:
        copy.wait_recv()
    xa = jnp.concatenate([xr[:, c].reshape(512, 128) for c in range(4)], axis=1)
    spread = dot(xa, perm[...]).astype(BF).reshape(16, 32, 512)
    for h in range(2):
        rows = spread[:, h * 16:(h + 1) * 16].reshape(256, 512)
        dv = (dot(k0[0], rows) + dot(k0[1], rows)).astype(BF)
        for ri in range(2):
            for i in range(4):
                dsc[:, pl.ds(ri * 128 + i * 32 + h * 16, 16), :] = dv[
                    ri * 512:(ri + 1) * 512, i * 128:(i + 1) * 128].reshape(32, 16, 128)

    def forward(t, carry):
        ecs = []
        for u in range(4):
            r = t * 4 + u
            e = dot(m[r], dsc[r])
            er, ei = e[:128], e[128:]
            c, s = tw[r, 0], tw[r, 1]
            ecs.append(jnp.concatenate([er * c + ei * s, ei * c - er * s], axis=1).astype(BF))
        for u in range(0, 4, 2):
            f = dot_nt(l2[...], jnp.concatenate(ecs[u:u + 2], axis=0))
            fsc[t * 4 + u] = f[:, :128]
            fsc[t * 4 + u + 1] = f[:, 128:]
        return carry

    lax.fori_loop(0, 8, forward, 0)
    for n in range(8, 14):
        loads[n].wait()
    low = lax.broadcasted_iota(jnp.int32, (32, 128), 1) < 64

    def inverse_of(g, qs):
        rs = [2 * q + i for q in qs for i in range(2)]
        ps = []
        for n, r in enumerate(rs):
            fr = fsc[r, pl.ds(g * 64, 64), :]
            fi = fsc[r, pl.ds(128 + g * 64, 64), :]
            re, im = hr[g, qs[n // 2], 0, n % 2].astype(F32), hr[g, qs[n // 2], 1, n % 2].astype(F32)
            ps.append(jnp.concatenate([fr * re - fi * im, fr * im + fi * re], axis=0).astype(BF))
        gv = [dot(l2i[...], jnp.concatenate(ps[n:n + 2], axis=1)) for n in range(0, len(rs), 2)]
        os = []
        for n, r in enumerate(rs):
            half = gv[n // 2][:, (n % 2) * 128:(n % 2 + 1) * 128]
            gr, gi = half[:64], half[64:]
            c, s = twi[r, 0], twi[r, 1]
            gc = jnp.concatenate([gr * c - gi * s, gi * c + gr * s], axis=1).astype(BF)
            os.append(dot_nt(mi[r], jnp.concatenate([gc, gc], axis=0)))
        for r, o in zip(rs, os):
            for ri in range(2):
                for k in range(2):
                    at = ri * 128 + k * 64
                    val = jnp.where(low, o[at:at + 32], o[at + 32:at + 64]).astype(BF)
                    for h in range(2):
                        osc[g, h, pl.ds(pl.multiple_of(ri * 512 + r * 16, 16), 16), pl.ds(k * 128, 128)] = (
                            val[h * 16:(h + 1) * 16])

    def inverse_step(g):
        def step(t, carry):
            for u in range(2):
                d = 2 * t + u
                pltpu.make_async_remote_copy(
                    src_ref=hs.at[g, d], dst_ref=hr.at[g, lax.rem(me - d + SEQ_N, SEQ_N)],
                    send_sem=hs_sem.at[g, d], recv_sem=hr_sem.at[g, d], device_id=(me, mc),
                    device_id_type=MESH).wait_recv()
            inverse_of(g, [lax.rem(me - 2 * t - u + SEQ_N, SEQ_N) for u in range(2)])
            return carry
        return step

    def inverse_first(g):
        filter_copy(g, 1).wait_recv()
        inverse_of(g, [me, source[1]])

    def inverse_end(g):
        for h in range(2):
            back = dot(k0i[0], osc[g, h]) + dot(k0i[1], osc[g, h])
            y = dot((back * (1.0 / N)).astype(BF), permi[...]).astype(BF).reshape(16, 16, 256)
            for cl in range(2):
                cs[g, :, cl, pl.ds(h * 16, 16), :] = y[:, :, cl * 128:(cl + 1) * 128]
        sent = []
        for d in range(1, SEQ_N):
            copy = pltpu.make_async_remote_copy(
                src_ref=cs.at[g, peer[d]], dst_ref=cr.at[g, me], send_sem=cs_sem.at[g, d],
                recv_sem=cr_sem.at[g, d], device_id=(peer[d], mc), device_id_type=MESH)
            copy.start()
            sent.append(copy)
        cr[g, me] = cs[g, me]
        return sent

    own, gathered, done = {}, [], []

    def gating(g, arrivals):
        for copy in arrivals:
            copy.wait_recv()
        for cl in range(2):
            c32[cl] = cr[g, :, cl].reshape(512, 128).astype(F32)
        width = 4096 // CHUNKS[g]
        for t in range(CHUNKS[g]):
            for cl in range(2):
                at = (2 * g + cl) * 16
                gain = gain_col[at:at + 16]
                for j in range(t * width // 128, (t + 1) * width // 128):
                    lanes = slice(j * 128, (j + 1) * 128)
                    direct = c32[cl, pl.ds(j, 16, stride=32), :] + gain * sig[at:at + 16, lanes].astype(F32)
                    gt[mz, g, pl.ds(cl * 16, 16), lanes] = (gate[at:at + 16, lanes].astype(F32) * direct).astype(BF)
            own[g, t] = [pass_on(g, t, mz, every, upc, 0), pass_on(g, t, mz, every, dnc, 1)]

    halves = {}
    every, first, second = pl.ds(0, 32), pl.ds(0, 16), pl.ds(16, 16)
    zdn, zup = lax.rem(mz + 3, 4), lax.rem(mz + 1, 4)

    def pass_on(g, t, block, rows, to, n):
        width = 4096 // CHUNKS[g]
        part = gt.at[block, g, rows, pl.ds(t * width, width)]
        copy = pltpu.make_async_remote_copy(
            src_ref=part, dst_ref=part, send_sem=gs_sem.at[g, t * 4 + n],
            recv_sem=gr_sem.at[g, t * 4 + n], device_id=(me, to), device_id_type=MESH)
        copy.start()
        gathered.append(copy)
        return copy

    def send_on(g, chunks):
        for t in chunks:
            own[g, t][0].wait_recv()
            own[g, t][1].wait_recv()
            halves[g, t] = [pass_on(g, t, zdn, first, upc, 2), pass_on(g, t, zup, second, dnc, 3)]

    at_k = lax.broadcasted_iota(jnp.int32, (512, 128), 0)
    at_n = lax.broadcasted_iota(jnp.int32, (512, 128), 1)

    def weights(g):
        pick = at_k == (at_n // 32) * 128 + xh * 64 + g * 32 + at_n % 32
        both = jnp.concatenate([w_ref[...], wp[...]], axis=0)
        return dot(both, jnp.where(pick, 1.0, 0.0).astype(BF)).astype(BF)

    def partial(g, wg, lanes):
        return dot(wg, gt[:, g, :, lanes].reshape(128, lanes.stop - lanes.start))

    filter_sent(0)
    start_filter(1)
    inverse_first(0)
    lax.fori_loop(1, 8, inverse_step(0), 0)
    conv_a = inverse_end(0)
    inverse_first(1)
    lax.fori_loop(1, SPLIT, inverse_step(1), 0)
    gating(0, conv_a)
    lax.fori_loop(SPLIT, 8, inverse_step(1), 0)
    conv_b = inverse_end(1)
    send_on(0, [0, 1])
    w_copy.wait_recv()
    w0, w1 = weights(0), weights(1)
    gating(1, conv_b)
    for copy in halves[0, 0] + halves[0, 1]:
        copy.wait_recv()
    for j in range(8):
        lanes = slice(j * 512, (j + 1) * 512)
        acc[:, lanes] = partial(0, w0, lanes)
    swaps = []
    send_on(1, [0])
    width = 4096 // CHUNKS[1]
    for t in range(CHUNKS[1]):
        if t + 1 < CHUNKS[1]:
            send_on(1, [t + 1])
        for copy in halves[1, t]:
            copy.wait_recv()
        lanes = slice(t * width, (t + 1) * width)
        full = acc[:, lanes] + partial(1, w1, lanes)
        acc[0:64, lanes] = full[:64]
        ps[:, lanes] = full[64:].astype(BF)
        part = pl.ds(t * width, width)
        copy = pltpu.make_async_remote_copy(
            src_ref=ps.at[:, part], dst_ref=pr.at[:, part], send_sem=ps_sem.at[t], recv_sem=pr_sem.at[t],
            device_id=(me, pc), device_id_type=MESH)
        copy.start()
        swaps.append(copy)
    stores = []
    for t, copy in enumerate(swaps):
        copy.wait_recv()
        lanes = slice(t * width, (t + 1) * width)
        out_ref[:, lanes] = (acc[0:64, lanes] + pr[:, lanes].astype(F32)).astype(BF)
        copy = pltpu.make_async_copy(out_ref.at[:, lanes], out_hbm.at[:, lanes], out_sem.at[t])
        copy.start()
        stores.append(copy)
    for copy in stores:
        copy.wait()
    filter_sent(1)
    for copy in conv_a + conv_b + gathered + swaps + [w_copy]:
        if id(copy) not in done:
            copy.wait_send()


def body(signal, gate, spec_real, spec_imag, skip_gain, mix_weight):
    consts = [jnp.asarray(v) for v in constants()]
    rows = lambda v: v.reshape(64, 2, 32, 128).transpose(0, 2, 1, 3).reshape(4096, 128)
    anywhere = pl.BlockSpec(memory_space=pl.ANY)
    vmem = pl.BlockSpec(memory_space=pltpu.VMEM)
    buf = lambda *shape: pltpu.VMEM(shape, BF)
    wide = lambda *shape: pltpu.VMEM(shape, F32)
    dma = lambda *shape: pltpu.SemaphoreType.DMA(shape)
    held = [pltpu.VMEM(v.shape, v.dtype) for v in consts]
    return pl.pallas_call(
        kernel,
        out_shape=jax.ShapeDtypeStruct((64, 4096), BF),
        in_specs=[anywhere] * 4 + [vmem, anywhere] + [anywhere] * len(consts),
        out_specs=anywhere,
        scratch_shapes=[buf(64, 512), buf(64, 4096), buf(64, 4096), buf(64, 4096), wide(2, 4096, 128)] + held + [
            wide(4, 512, 128), buf(16, 4, 32, 128), buf(16, 4, 32, 128),
            buf(2, 16, 2, 2, 64, 128), buf(2, 16, 2, 2, 64, 128), buf(32, 256, 128), wide(32, 256, 128),
            buf(2, 2, 1024, 256), buf(2, 16, 2, 32, 128), buf(2, 16, 2, 32, 128), wide(2, 512, 128),
            buf(4, 2, 32, 4096), buf(64, 512), wide(128, 4096), buf(64, 4096), buf(64, 4096),
            dma(15), dma(16), dma(16), dma(2, 16), dma(2, 16), dma(2, 16), dma(2, 16), dma(2, 16), dma(2, 16), dma(5), dma(5), dma(4)],
        compiler_params=pltpu.CompilerParams(
            collective_id=0, has_side_effects=True, vmem_limit_bytes=60 * 1024 * 1024),
        cost_estimate=pl.CostEstimate(flops=10**10, bytes_accessed=3 * 10**7, transcendentals=0),
    )(signal, gate, rows(spec_real), rows(spec_imag), skip_gain.reshape(1, 64), mix_weight, *consts)


def solution(mesh):
    placed = (
        P("chan", "seq"),
        P("chan", "seq"),
        P("chan", "seq", None),
        P("chan", "seq", None),
        P("chan"),
        P("chan", None),
    )
    return jax.shard_map(
        body, mesh=mesh, in_specs=placed, out_specs=P("chan", "seq"), check_vma=False
    )
```
